128 devices in a mesh: elem: 8 (over x, core), mode: 16 (over z, y).
Axes of the slice: x: 4, y: 4, z: 4, core: 2. Of those that a mesh axis runs over, the one named last changes fastest.
Arguments:
- velocity: float32 [3, 2, 256, 64, 1024], P(None, None, 'mode', None, 'elem'), may hold values from -0.625 to 0.625
- metric: float32 [4, 64, 1024], P(None, None, 'elem'), may hold values from -2 to 2
- mass: float32 [64, 1024], P(None, 'elem'), may hold values from 0.3 to 4.5
- sponge_rate: float32 [64, 1024], P(None, 'elem'), may hold values from 0.5 to 4
- sponge_mask: int32 [1024], P('elem'), may hold values 0 or 1
- neighbours: int32 [4, 1024], P(None, 'elem'), may hold values from -1 to 1023, as said below
Outputs:
- nonlinear: float32 [3, 2, 256, 64, 1024], P(None, None, 'mode', None, 'elem')
- pressure: float32 [2, 256, 64, 1024], P(None, 'mode', None, 'elem')
The draws below stay inside these ranges and needn't reach their ends.
Inputs may be any that keep to these rules, and one draw needn't show every extreme that they name: Rows are the west, east, south and north neighbour of each element, -1 where there is none. The elements form one grid of 16 rows; relations are mutual; north and south neighbours lie on the same index of elem, east and west ones on the same or an adjacent index; the south neighbour of the west neighbour is the west neighbour of the south neighbour, and likewise at all four corners.
All inputs are finite; a program needn't handle non-finite values. No bound on the sum of `sponge_mask` on one device may be relied on, other than what follows from the above.
Results may differ from the reference program's by a relative error of at most 0.00013.
Values sent between devices are 32-bit elements; how exact they have to be, the bound alone decides.
No kernel may reach another device: no remote copies, remote signals or barrier semaphores. Data moves between devices by JAX's collectives and lax.ppermute only.
A program may use at most 192 MiB of HBM per device.

```python
import math
import jax
import jax.numpy as jnp
import numpy as np
from jax import lax

MODES = 256
NODES = 64
ELEM_DEV = 128
GRID_ROWS = 16
ITERS = 2
ELEMENTS = 1024


def draw_mass(key, part):
    key = jax.random.fold_in(key, 5)
    devices = ELEMENTS // ELEM_DEV
    column = (jnp.arange(ELEMENTS) // ELEM_DEV).astype(jnp.float32)
    rise = 1.0 + 2.0 * column / max(devices - 1, 1)
    base = jnp.exp(jax.random.uniform(key, (NODES, ELEMENTS), jnp.float32, jnp.log(0.3), jnp.log(1.5)))
    return (base * rise[None, :]).astype(jnp.float32)


def shuffle_slots(single):
    return jax.random.permutation(single, ELEM_DEV)


def draw_neighbours(key, part):
    key = jax.random.fold_in(key, 11)
    devices = ELEMENTS // ELEM_DEV
    across = ELEM_DEV // GRID_ROWS
    total_columns = devices * across
    keys = jax.random.split(key, devices)
    slots = jax.vmap(shuffle_slots)(keys)
    cells = jnp.argsort(slots, axis=1)
    owner = jnp.arange(devices)[:, None]
    row = cells // across
    column = owner * across + cells % across

    def ident(row_at, column_at):
        valid = (row_at >= 0) & (row_at < GRID_ROWS) & (column_at >= 0) & (column_at < total_columns)
        row_safe = jnp.clip(row_at, 0, GRID_ROWS - 1)
        column_safe = jnp.clip(column_at, 0, total_columns - 1)
        home = column_safe // across
        picked = slots[home, row_safe * across + column_safe % across]
        return jnp.where(valid, home * ELEM_DEV + picked, -1)
    links = jnp.stack([ident(row, column - 1), ident(row, column + 1), ident(row - 1, column), ident(row + 1, column)])
    return links.reshape(4, ELEMENTS).astype(jnp.int32)


def with_ends(array, own_key, low, high):
    spot = [jax.random.randint(jax.random.fold_in(own_key, axis), (), 0, length) for axis, length in enumerate(array.shape)]
    main_axis = array.shape.index(max(array.shape))
    neighbour = spot[:main_axis] + [(spot[main_axis] + 1) % array.shape[main_axis]] + spot[main_axis + 1:]
    return array.at[tuple(spot)].set(low).at[tuple(neighbour)].set(high)


def block_scale(rng, extent, pieces, low, largest):
    loudness = 1.0
    for position, parts in pieces:
        heights = jax.random.uniform(jax.random.fold_in(jax.random.fold_in(rng, 6), position), (parts,), jnp.float32, low / len(pieces), largest / len(pieces))
        loudness = loudness * jnp.repeat(jnp.exp(heights), extent[position] // parts).reshape((-1,) + (1,) * (len(extent) - 1 - position))
    return loudness


def centred(stream_key, shape, width, reach, cuts=(), kind=jnp.bfloat16):
    array = jax.random.normal(stream_key, shape, jnp.float32) * width
    if len(cuts) > 0:
        array = block_scale(stream_key, shape, cuts, -0.22, 0.18) * array
    return jnp.clip(array, min=-reach, max=reach).astype(kind)


def setup_inputs(seed: int = 0) -> dict:
    key_of = jax.random.split(jax.random.key(seed), 7)
    velocity = centred(key_of[0], (3, 2, MODES, NODES, ELEMENTS), ((2 * MODES) ** -0.5), 0.625, ((2, 16), (4, 8)), jnp.float32)
    metric = centred(key_of[1], (4, NODES, ELEMENTS), 0.15, 2.0, ((2, 8),), jnp.float32)
    mass = draw_mass(jax.random.fold_in(key_of[6], 71), 0)
    sponge_rate = jnp.clip(jnp.exp(math.log(4.0) - 2.0794415 * jax.random.uniform(key_of[3], (NODES, ELEMENTS), jnp.float32) ** block_scale(key_of[3], (NODES, ELEMENTS), ((1, 8),), -0.2, 0.2)), 0.5, 4.0)
    sponge_mask = with_ends((jax.random.randint(key_of[4], (ELEMENTS,), 0, 3) < 1).astype(jnp.int32), jax.random.fold_in(key_of[4], 1), 0, 1)
    neighbours = draw_neighbours(jax.random.fold_in(key_of[6], 71), 0)
    return {"velocity": velocity, "metric": metric, "mass": mass, "sponge_rate": sponge_rate, "sponge_mask": sponge_mask, "neighbours": neighbours}


def cheb_matrix():
    count = 8
    places = np.arange(count)
    points = np.cos(np.pi * places / (count - 1))
    weights = np.where((places == 0) | (places == count - 1), 2.0, 1.0)
    signs = weights * (-1.0) ** places
    differ = points[:, None] - points[None, :] + np.eye(count)
    table = np.outer(signs, 1.0 / signs) / differ
    table = table - np.eye(count) * np.sum(table, axis=1)[:, None]
    return jnp.asarray(table, dtype=jnp.float32)

def node_grads(field, table):
    shape = field.shape
    grid = field.reshape(shape[:-2] + (8, 8, shape[-1]))
    along_r = jnp.einsum('bc,...ace->...abe', table, grid, precision=lax.Precision.HIGHEST)
    along_s = jnp.einsum('ac,...cbe->...abe', table, grid, precision=lax.Precision.HIGHEST)
    return (along_r.reshape(shape), along_s.reshape(shape))

def node_grads_adjoint(first, second, table):
    shape = first.shape
    grid_r = first.reshape(shape[:-2] + (8, 8, shape[-1]))
    grid_s = second.reshape(shape[:-2] + (8, 8, shape[-1]))
    back_r = jnp.einsum('cb,...ace->...abe', table, grid_r, precision=lax.Precision.HIGHEST)
    back_s = jnp.einsum('ca,...cbe->...abe', table, grid_s, precision=lax.Precision.HIGHEST)
    return (back_r + back_s).reshape(shape)

def plane_grads(field, metric, table):
    along_r, along_s = node_grads(field, table)
    return (metric[0] * along_r + metric[2] * along_s, metric[1] * along_r + metric[3] * along_s)

def stiffness(field, metric, mass, shift, table):
    grad_x, grad_y = plane_grads(field, metric, table)
    flux_x = mass * grad_x
    flux_y = mass * grad_y
    folded = node_grads_adjoint(metric[0] * flux_x + metric[1] * flux_y, metric[2] * flux_x + metric[3] * flux_y, table)
    return folded + shift * mass * field

def span_grad(field, wave):
    return jnp.stack([-wave * field[..., 1, :, :, :], wave * field[..., 0, :, :, :]], axis=-4)

def vorticity(field, metric, wave, table):
    grad_x, grad_y = plane_grads(field, metric, table)
    return jnp.stack([grad_y[2] - span_grad(field[1], wave), span_grad(field[0], wave) - grad_x[2], grad_x[1] - grad_y[0]])

def forcing(speed, swirl, damping):
    return jnp.stack([speed[1] * swirl[2] - speed[2] * swirl[1] - damping * (speed[0] - 1.0), speed[2] * swirl[0] - speed[0] * swirl[2] - damping * speed[1], speed[0] * swirl[1] - speed[1] * swirl[0] - damping * speed[2]])

def to_planes(coeff):
    spectrum = coeff[..., 0, :, :, :] + 1j * coeff[..., 1, :, :, :]
    padded = jnp.concatenate([spectrum, jnp.zeros_like(spectrum[..., :1, :, :])], axis=-3)
    return jnp.fft.irfft(padded, n=2 * MODES, axis=-3) * (2 * MODES)

def from_planes(values):
    spectrum = jnp.fft.rfft(values, axis=-3)[..., :MODES, :, :] / (2 * MODES)
    return jnp.stack([spectrum.real, spectrum.imag], axis=-4)

def partner(values, index):
    present = index >= 0
    picked = jnp.take(values, jnp.where(present, index, 0), axis=-1)
    return picked * present.astype(values.dtype)

def shared_sum(field, neighbours):
    shape = field.shape
    grid = field.reshape(shape[:-2] + (8, 8, shape[-1]))
    first = grid[..., :, 0, :] + partner(grid[..., :, 7, :], neighbours[0])
    last = grid[..., :, 7, :] + partner(grid[..., :, 0, :], neighbours[1])
    grid = jnp.concatenate([first[..., :, None, :], grid[..., :, 1:7, :], last[..., :, None, :]], axis=-2)
    bottom = grid[..., 0, :, :] + partner(grid[..., 7, :, :], neighbours[2])
    top = grid[..., 7, :, :] + partner(grid[..., 0, :, :], neighbours[3])
    grid = jnp.concatenate([bottom[..., None, :, :], grid[..., 1:7, :, :], top[..., None, :, :]], axis=-3)
    return grid.reshape(shape)

def reference(velocity, metric, mass, sponge_rate, sponge_mask, neighbours):
    table = cheb_matrix()
    wave = (jnp.arange(MODES).astype(jnp.float32) * (jnp.pi / MODES)).astype(jnp.float32)
    wave_all = wave[:, None, None]
    block = 16

    def nonlinear_block(index, result):
        start = (index * block).astype(jnp.int32)
        field = lax.dynamic_slice_in_dim(velocity, start, block, axis=4)
        local_metric = lax.dynamic_slice_in_dim(metric, start, block, axis=2)
        rate = lax.dynamic_slice_in_dim(sponge_rate, start, block, axis=1)
        flags = lax.dynamic_slice_in_dim(sponge_mask, start, block, axis=0)
        swirl = vorticity(field, local_metric, wave_all, table)
        speed = to_planes(field)
        swirl_planes = to_planes(swirl)
        damping = flags.astype(jnp.float32)[None, :] * rate
        force = forcing(speed, swirl_planes, damping)
        return lax.dynamic_update_slice_in_dim(result, from_planes(force).astype(jnp.float32), start, axis=4)
    nonlinear = lax.fori_loop(0, ELEMENTS // block, nonlinear_block, jnp.zeros(velocity.shape, jnp.float32))
    multiplicity = shared_sum(jnp.ones((NODES, ELEMENTS), jnp.float32), neighbours)
    mode_block = 16

    def pressure_block(index, result):
        start = (index * mode_block).astype(jnp.int32)
        group = lax.dynamic_slice_in_dim(nonlinear, start, mode_block, axis=2)
        wave_part = lax.dynamic_slice_in_dim(wave, start, mode_block, axis=0)[:, None, None]
        shift = wave_part * wave_part + 1.0
        grad_x0 = plane_grads(group[0], metric, table)[0]
        grad_y1 = plane_grads(group[1], metric, table)[1]
        divergence = grad_x0 + grad_y1 + span_grad(group[2], wave_part)
        right = shared_sum(-mass * divergence, neighbours)

        def inner(first, second):
            return lax.optimization_barrier(jnp.sum(first * second / multiplicity, axis=(0, 2, 3)))[:, None, None]
        solution = jnp.zeros_like(right)
        residual = right
        direction = right
        norm_now = inner(residual, residual)
        for sweep in range(ITERS):
            image = shared_sum(stiffness(direction, metric, mass, shift, table), neighbours)
            alpha = norm_now / inner(direction, image)
            solution = solution + alpha * direction
            residual = residual - alpha * image
            norm_next = inner(residual, residual)
            direction = residual + norm_next / norm_now * direction
            norm_now = norm_next
        return lax.dynamic_update_slice_in_dim(result, solution, start, axis=1)
    pressure = lax.fori_loop(0, MODES // mode_block, pressure_block, jnp.zeros((2, MODES, NODES, ELEMENTS), jnp.float32))
    return (nonlinear, pressure)
```

```python
import jax
import jax.numpy as jnp
import ml_dtypes
import numpy as np
from jax import lax
from jax.experimental import pallas as pl
from jax.experimental.pallas import tpu as pltpu
from jax.sharding import PartitionSpec as P

F32 = jnp.float32
BF16 = jnp.bfloat16
LIMIT = 50 * 1024 * 1024


def cheb_matrix():
    count = 8
    places = np.arange(count)
    points = np.cos(np.pi * places / (count - 1))
    weights = np.where((places == 0) | (places == count - 1), 2.0, 1.0)
    signs = weights * (-1.0) ** places
    differ = points[:, None] - points[None, :] + np.eye(count)
    table = np.outer(signs, 1.0 / signs) / differ
    table = table - np.eye(count) * np.sum(table, axis=1)[:, None]
    return table.astype(np.float32).astype(np.float64)


def two_parts(table):
    high = table.astype(np.float32).astype(ml_dtypes.bfloat16)
    low = (table - high.astype(np.float64)).astype(np.float32).astype(ml_dtypes.bfloat16)
    return high, low


def tables(modes):
    planes = 2 * modes
    order = np.arange(modes)
    spots = np.arange(modes)
    phase = (spots[:, None] * order[None, :]) % planes
    angle = phase * (2.0 * np.pi / planes)
    weight = np.where(order == 0, 1.0, 2.0)
    cosine = np.cos(angle)
    sine = np.sin(angle)
    last = np.zeros((16, modes))
    last[0] = weight * (-1.0) ** order
    synth_cos = np.concatenate([weight * cosine, last], axis=0)
    synth_sin = weight * sine
    back_cos = cosine.T / planes
    back_sin = -sine.T / planes
    wave = np.broadcast_to((order * np.pi / modes)[:, None], (modes, 128)).astype(np.float32)
    sign = np.broadcast_to(((-1.0) ** order / planes)[:, None], (modes, 128)).astype(np.float32)
    return synth_cos, synth_sin, back_cos, back_sin, wave, sign


def right_tables():
    table = cheb_matrix()
    two = np.eye(2)
    eight = np.eye(8)
    along_r = np.kron(two, np.kron(eight, table.T))
    along_s = np.kron(two, np.kron(table.T, eight))
    both = np.concatenate([along_r, along_s], axis=1)
    high, low = two_parts(both)
    return np.concatenate([high, high], axis=0), low


def left_tables():
    table = cheb_matrix()
    eight = np.eye(8)
    along_r = np.kron(eight, table)
    along_s = np.kron(table, eight)
    high, low = two_parts(np.concatenate([along_r, along_s], axis=0))
    forward = np.concatenate([high, high, low], axis=1)
    high, low = two_parts(np.concatenate([along_r.T, along_s.T], axis=1))
    return forward, np.concatenate([high, high], axis=1), low


def split(value):
    high = value.astype(BF16)
    low = (value - high.astype(F32)).astype(BF16)
    return high, low


def dot(first, second):
    return jnp.dot(first, second, preferred_element_type=F32)


def low_half(shape):
    return lax.broadcasted_iota(jnp.int32, shape, len(shape) - 1) < 64


def swap(value):
    return pltpu.roll(value, 64, 1)


def pre_kernel(v_ref, y_ref, tmp):
    for kl in range(16):
        block = v_ref[0, :, kl].reshape(128, 128)
        tmp[pl.ds(kl, 128, stride=16), :] = block.T
    half = low_half((16, 128))
    for pair in range(64):
        first = tmp[32 * pair : 32 * pair + 16, :]
        second = tmp[32 * pair + 16 : 32 * pair + 32, :]
        g, i = divmod(pair, 4)
        cols = slice(128 * i, 128 * i + 128)
        y_ref[g, 0, 0, :, cols] = jnp.where(half, first, swap(second))
        y_ref[g, 0, 1, :, cols] = jnp.where(half, swap(first), second)


def to_blocks(velocity):
    return pl.pallas_call(
        pre_kernel,
        grid=(3,),
        in_specs=[pl.BlockSpec((1, 2, 16, 64, 128), lambda c: (c, 0, 0, 0, 0))],
        out_specs=pl.BlockSpec((16, 1, 2, 16, 512), lambda c: (0, c, 0, 0, 0)),
        out_shape=jax.ShapeDtypeStruct((16, 3, 2, 16, 512), F32),
        scratch_shapes=[pltpu.VMEM((2048, 128), F32)],
        compiler_params=pltpu.CompilerParams(vmem_limit_bytes=LIMIT),
        name="to_blocks",
    )(velocity)


ROWS = 32


def plane_kernel(
    z_ref, rows_ref, wave_ref, sign_ref, wst_ref, wlo_ref, ch_ref, cl_ref, sh_ref, sl_ref,
    bch_ref, bcl_ref, bsh_ref, bsl_ref, out_ref, high, low, planes, eh, el, tail,
):
    rx = rows_ref[0:1, :]
    ry = rows_ref[1:2, :]
    sx = rows_ref[2:3, :]
    sy = rows_ref[3:4, :]
    damping = rows_ref[4:5, :]
    count = ROWS // 16

    def curls(step, carry):
        rows = pl.ds(pl.multiple_of(step * ROWS, ROWS), ROWS)
        wave = jnp.concatenate([wave_ref[rows, :]] * 2, axis=1)
        fields = {}
        slopes = {}
        for c in range(3):
            for part in range(2):
                value = z_ref[pl.ds(step * count, count), c, part].reshape(ROWS, 256)
                up, down = split(value)
                high[c, part, rows, :] = up
                low[c, part, rows, :] = down
                fields[c, part] = value
                pieces = []
                for q in range(2):
                    cols = slice(128 * q, 128 * q + 128)
                    both = jnp.concatenate([up[:, cols], down[:, cols]], axis=1)
                    pieces.append(dot(both, wst_ref[...]) + dot(up[:, cols], wlo_ref[...]))
                slopes[c, part] = (
                    jnp.concatenate([pieces[0][:, :128], pieces[1][:, :128]], axis=1),
                    jnp.concatenate([pieces[0][:, 128:], pieces[1][:, 128:]], axis=1),
                )
        for part in range(2):
            u_r, u_s = slopes[0, part]
            v_r, v_s = slopes[1, part]
            w_r, w_s = slopes[2, part]
            if part == 0:
                dz_u = -wave * fields[0, 1]
                dz_v = -wave * fields[1, 1]
            else:
                dz_u = wave * fields[0, 0]
                dz_v = wave * fields[1, 0]
            swirl = (
                ry * w_r + sy * w_s - dz_v,
                dz_u - (rx * w_r + sx * w_s),
                rx * v_r + sx * v_s - (ry * u_r + sy * u_s),
            )
            for c in range(3):
                up, down = split(swirl[c])
                high[3 + c, part, rows, :] = up
                low[3 + c, part, rows, :] = down
        return carry

    lax.fori_loop(0, 256 // ROWS, curls, 0)

    def synth(c, carry):
        re_h = high[c, 0]
        re_l = low[c, 0]
        im_h = high[c, 1]
        im_l = low[c, 1]
        even = dot(ch_ref[...], re_h) + dot(ch_ref[...], re_l) + dot(cl_ref[...], re_h)
        odd = dot(sh_ref[...], im_h) + dot(sh_ref[...], im_l) + dot(sl_ref[...], im_h)
        planes[c, 0] = even[:256] - odd
        planes[c, 1] = even[:256] + odd
        planes[c, 1, 0:1, :] = even[256:257, :]
        return carry

    lax.fori_loop(0, 6, synth, 0)

    def force(u, w):
        return (
            u[1] * w[2] - u[2] * w[1] - damping * (u[0] - 1.0),
            u[2] * w[0] - u[0] * w[2] - damping * u[1],
            u[0] * w[1] - u[1] * w[0] - damping * u[2],
        )

    def forces(step, carry):
        rows = pl.ds(pl.multiple_of(step * ROWS, ROWS), ROWS)
        front = [planes[c, 0, rows, :] for c in range(6)]
        back = [planes[c, 1, rows, :] for c in range(6)]
        front = force(front[:3], front[3:])
        back = force(back[:3], back[3:])
        place = lax.broadcasted_iota(jnp.int32, (ROWS, 256), 0) + step * ROWS
        for c in range(3):
            kept = jnp.where(place == 0, 0.0, back[c])
            up, down = split(front[c] + kept)
            eh[c, 0, rows, :] = up
            el[c, 0, rows, :] = down
            up, down = split(front[c] - kept)
            eh[c, 1, rows, :] = up
            el[c, 1, rows, :] = down

        @pl.when(step == 0)
        def _():
            for c in range(3):
                tail[c, 0:8, :] = back[c][0:8, :]

        return carry

    lax.fori_loop(0, 256 // ROWS, forces, 0)

    def analyse(c, carry):
        e_h = eh[c, 0]
        e_l = el[c, 0]
        o_h = eh[c, 1]
        o_l = el[c, 1]
        re = dot(bch_ref[...], e_h) + dot(bch_ref[...], e_l) + dot(bcl_ref[...], e_h)
        im = dot(bsh_ref[...], o_h) + dot(bsh_ref[...], o_l) + dot(bsl_ref[...], o_h)
        sign = jnp.concatenate([sign_ref[...]] * 2, axis=1)
        re = re + sign * tail[c, 0:1, :]
        out_ref[:, c, 0] = re.reshape(16, 16, 256)
        out_ref[:, c, 1] = im.reshape(16, 16, 256)
        return carry

    lax.fori_loop(0, 3, analyse, 0)


def in_planes(blocks, rows):
    synth_cos, synth_sin, back_cos, back_sin, wave, sign = tables(256)
    wst, wlo = right_tables()
    consts = [wave, sign, wst, wlo]
    for table in (synth_cos, synth_sin, back_cos, back_sin):
        consts.extend(two_parts(table))
    consts = [jnp.asarray(c) for c in consts]

    def whole(array):
        return pl.BlockSpec(array.shape, lambda i: (0,) * array.ndim)

    block = pl.BlockSpec((16, 3, 2, 16, 256), lambda i: (0, 0, 0, 0, i))
    return pl.pallas_call(
        plane_kernel,
        grid=(2,),
        in_specs=[block, pl.BlockSpec((8, 256), lambda i: (0, i))] + [whole(c) for c in consts],
        out_specs=block,
        out_shape=jax.ShapeDtypeStruct((16, 3, 2, 16, 512), F32),
        scratch_shapes=[
            pltpu.VMEM((6, 2, 256, 256), BF16),
            pltpu.VMEM((6, 2, 256, 256), BF16),
            pltpu.VMEM((6, 2, 256, 256), F32),
            pltpu.VMEM((3, 2, 256, 256), BF16),
            pltpu.VMEM((3, 2, 256, 256), BF16),
            pltpu.VMEM((3, 8, 256), F32),
        ],
        compiler_params=pltpu.CompilerParams(vmem_limit_bytes=LIMIT),
        name="in_planes",
    )(blocks, rows, *consts)


def slopes_of(pair, forward):
    up, down = split(pair)
    both = dot(forward, jnp.concatenate([up, down, up], axis=0))
    return both[:64], both[64:]


def twice(value):
    return jnp.concatenate([value, value], axis=1)


def post_kernel(r_ref, wave_ref, coef_ref, fwd_ref, non_ref, raw_ref, edge_ref, tmp):
    half = low_half((8, 128))
    for c in range(3):
        for pair in range(64):
            g, i = divmod(pair, 4)
            cols = slice(128 * i, 128 * i + 128)
            re = r_ref[g, c, 0, :, cols]
            im = r_ref[g, c, 1, :, cols]
            tmp[c, 16 * pair : 16 * pair + 8, :] = jnp.where(half, re, swap(im))
            tmp[c, 16 * pair + 8 : 16 * pair + 16, :] = jnp.where(half, swap(re), im)
    base = pl.program_id(0) * 8
    for kl in range(8):
        cells = []
        for c in range(3):
            block = tmp[c, pl.ds(kl, 128, stride=8), :].T
            non_ref[c, :, kl] = block.reshape(2, 64, 128)
            cells.append(block)
        x_r, x_s = slopes_of(jnp.concatenate([cells[0][:64], cells[0][64:]], axis=1), fwd_ref[...])
        y_r, y_s = slopes_of(jnp.concatenate([cells[1][:64], cells[1][64:]], axis=1), fwd_ref[...])
        wave = wave_ref[pl.ds(base + kl, 1), :]
        scaled = wave * coef_ref[0]
        for part in range(2):
            cols = slice(128 * part, 128 * part + 128)
            value = (
                coef_ref[1] * x_r[:, cols]
                + coef_ref[2] * x_s[:, cols]
                + coef_ref[3] * y_r[:, cols]
                + coef_ref[4] * y_s[:, cols]
            )
            if part == 0:
                value = value + scaled * cells[2][64:]
            else:
                value = value - scaled * cells[2][:64]
            raw_ref[part, kl] = value
            edge_ref[0, part, kl] = raw_ref[part, kl, pl.ds(0, 8, stride=8), :]
            edge_ref[1, part, kl] = raw_ref[part, kl, pl.ds(7, 8, stride=8), :]


def whole_spec(shape):
    return pl.BlockSpec(shape, lambda i: (0,) * len(shape))


FIELD = (2, 16, 64, 128)
EDGE = (2, 2, 16, 8, 128)


def from_blocks(blocks, wave, coef, forward):
    return pl.pallas_call(
        post_kernel,
        grid=(2,),
        in_specs=[
            pl.BlockSpec((16, 3, 2, 8, 512), lambda i: (0, 0, 0, i, 0)),
            whole_spec(wave.shape),
            whole_spec(coef.shape),
            whole_spec(forward.shape),
        ],
        out_specs=[
            pl.BlockSpec((3, 2, 8, 64, 128), lambda i: (0, 0, i, 0, 0)),
            pl.BlockSpec((2, 8, 64, 128), lambda i: (0, i, 0, 0)),
            pl.BlockSpec((2, 2, 8, 8, 128), lambda i: (0, 0, i, 0, 0)),
        ],
        out_shape=[
            jax.ShapeDtypeStruct((3, 2, 16, 64, 128), F32),
            jax.ShapeDtypeStruct(FIELD, F32),
            jax.ShapeDtypeStruct(EDGE, F32),
        ],
        scratch_shapes=[pltpu.VMEM((3, 1024, 128), F32)],
        compiler_params=pltpu.CompilerParams(vmem_limit_bytes=LIMIT),
        name="from_blocks",
    )(blocks, wave, coef, forward)


def lanes(value, index):
    return jnp.take_along_axis(value, index, axis=1, mode="promise_in_bounds")


def share(out_ref, field_ref, west_ref, east_ref, link_ref, part, kl):
    west_lane, west_from = link_ref[0], link_ref[1]
    east_lane, east_from = link_ref[2], link_ref[3]
    south_lane, south_here = link_ref[4], link_ref[5]
    north_lane, north_here = link_ref[6], link_ref[7]
    first = field_ref[part, kl, pl.ds(0, 8, stride=8), :]
    last = field_ref[part, kl, pl.ds(7, 8, stride=8), :]

    def pick(side, own, lane, origin):
        value = jnp.where(origin == 1, lanes(own, lane), 0.0)
        value = jnp.where(origin == 0, lanes(west_ref[side, part, kl], lane), value)
        return jnp.where(origin == 2, lanes(east_ref[side, part, kl], lane), value)

    out_ref[part, kl] = field_ref[part, kl]
    out_ref[part, kl, pl.ds(0, 8, stride=8), :] = first + pick(1, last, west_lane, west_from)
    out_ref[part, kl, pl.ds(7, 8, stride=8), :] = last + pick(0, first, east_lane, east_from)
    bottom = out_ref[part, kl, 0:8, :]
    top = out_ref[part, kl, 56:64, :]
    out_ref[part, kl, 0:8, :] = bottom + jnp.where(south_here == 1, lanes(top, south_lane), 0.0)
    out_ref[part, kl, 56:64, :] = top + jnp.where(north_here == 1, lanes(bottom, north_lane), 0.0)


def apply_stiffness(pair, shift, stiff_ref, fwd_ref, adj_ref, adl_ref):
    along_r, along_s = slopes_of(pair, fwd_ref[...])
    cross = twice(stiff_ref[1])
    back = jnp.concatenate(
        [
            twice(stiff_ref[0]) * along_r + cross * along_s,
            cross * along_r + twice(stiff_ref[2]) * along_s,
        ],
        axis=0,
    )
    up, down = split(back)
    folded = dot(adj_ref[...], jnp.concatenate([up, down], axis=0)) + dot(adl_ref[...], up)
    return folded + shift * twice(stiff_ref[3]) * pair


def image_kernel(
    raw_ref, west_ref, east_ref, link_ref, wave_ref, stiff_ref, fwd_ref, adj_ref, adl_ref,
    field_ref, image_ref, *rest, first,
):
    width = raw_ref.shape[1]
    base = pl.program_id(0) * width

    def body(kl, carry):
        for part in range(2):
            share(field_ref, raw_ref, west_ref, east_ref, link_ref, part, kl)
        pair = jnp.concatenate([field_ref[0, kl], field_ref[1, kl]], axis=1)
        wave = wave_ref[pl.ds(base + kl, 1), :]
        shift = twice(wave * wave + 1.0)
        image = apply_stiffness(pair, shift, stiff_ref, fwd_ref, adj_ref, adl_ref)
        image_ref[0, kl] = image[:, :128]
        image_ref[1, kl] = image[:, 128:]
        if first:
            edge_ref, sum_ref = rest
            for part in range(2):
                edge_ref[0, part, kl] = image_ref[part, kl, pl.ds(0, 8, stride=8), :]
                edge_ref[1, part, kl] = image_ref[part, kl, pl.ds(7, 8, stride=8), :]
            weighed = pair * pair * twice(stiff_ref[4])
            weighed = weighed[:, :128] + weighed[:, 128:]
            energy = pair * image
            energy = energy[:, :128] + energy[:, 128:]
            sum_ref[0, pl.ds(base + kl, 1), :] = jnp.sum(weighed, axis=0, keepdims=True)
            sum_ref[1, pl.ds(base + kl, 1), :] = jnp.sum(energy, axis=0, keepdims=True)
        return carry

    lax.fori_loop(0, width, body, 0)


def image_of(raw, west, east, links, wave, stiff, tables_left, first):
    pieces = 2
    width = 16 // pieces
    field_spec = pl.BlockSpec((2, width, 64, 128), lambda i: (0, i, 0, 0))
    edge_spec = pl.BlockSpec((2, 2, width, 8, 128), lambda i: (0, 0, i, 0, 0))
    out_specs = [field_spec, field_spec]
    out_shape = [jax.ShapeDtypeStruct(FIELD, F32)] * 2
    if first:
        out_specs += [edge_spec, whole_spec((2, 16, 128))]
        out_shape += [jax.ShapeDtypeStruct(EDGE, F32), jax.ShapeDtypeStruct((2, 16, 128), F32)]

    def kernel(*refs):
        image_kernel(*refs, first=first)

    return pl.pallas_call(
        kernel,
        grid=(pieces,),
        in_specs=[field_spec, edge_spec, edge_spec]
        + [whole_spec(a.shape) for a in (links, wave, stiff) + tuple(tables_left)],
        out_specs=out_specs,
        out_shape=out_shape,
        compiler_params=pltpu.CompilerParams(vmem_limit_bytes=LIMIT),
        name="image_first" if first else "image_second",
    )(raw, west, east, links, wave, stiff, *tables_left)


def totals(sum_ref):
    total = sum_ref[0]
    for d in range(1, sum_ref.shape[0]):
        total = total + sum_ref[d]
    return jnp.broadcast_to(jnp.sum(total, axis=-1, keepdims=True), total.shape)


def residual_kernel(field_ref, image_ref, shared_ref, second_ref, sum_ref, stiff_ref, out_ref, alpha):
    total = totals(sum_ref)
    alpha[...] = total[0] / total[1]

    def body(kl, carry):
        step = alpha[pl.ds(kl, 1), :]
        norm = jnp.zeros((64, 128), F32)
        energy = jnp.zeros((64, 128), F32)
        for part in range(2):
            residual = field_ref[part, kl] - step * shared_ref[part, kl]
            image = image_ref[part, kl] - step * second_ref[part, kl]
            norm = norm + residual * residual
            energy = energy + residual * image
        norm = norm * stiff_ref[4]
        out_ref[0, pl.ds(kl, 1), :] = jnp.sum(norm, axis=0, keepdims=True)
        out_ref[1, pl.ds(kl, 1), :] = jnp.sum(energy, axis=0, keepdims=True)
        return carry

    lax.fori_loop(0, 16, body, 0)


def residual_sums(field, image, shared, second, sums, stiff):
    return pl.pallas_call(
        residual_kernel,
        out_shape=jax.ShapeDtypeStruct((2, 16, 128), F32),
        scratch_shapes=[pltpu.VMEM((16, 128), F32)],
        compiler_params=pltpu.CompilerParams(vmem_limit_bytes=LIMIT),
        name="residual_sums",
    )(field, image, shared, second, sums, stiff)


def final_kernel(field_ref, shared_ref, sum_ref, next_ref, out_ref, scales):
    total = totals(sum_ref)
    norm0, energy0 = total[0], total[1]
    total = totals(next_ref)
    norm1, energy1 = total[0], total[1]
    alpha0 = norm0 / energy0
    beta = norm1 / norm0
    alpha1 = norm1 / (energy1 - beta * norm1 / alpha0)
    scales[0] = alpha0 + alpha1 * (1.0 + beta)
    scales[1] = -alpha1 * alpha0

    def body(kl, carry):
        one = scales[0, pl.ds(kl, 1), :]
        two = scales[1, pl.ds(kl, 1), :]
        for part in range(2):
            out_ref[part, kl] = one * field_ref[part, kl] + two * shared_ref[part, kl]
        return carry

    lax.fori_loop(0, 16, body, 0)


def final(field, shared, sums, later):
    return pl.pallas_call(
        final_kernel,
        out_shape=jax.ShapeDtypeStruct(FIELD, F32),
        scratch_shapes=[pltpu.VMEM((2, 16, 128), F32)],
        compiler_params=pltpu.CompilerParams(vmem_limit_bytes=LIMIT),
        name="pressure",
    )(field, shared, sums, later)


def link_tables(neighbours, width):
    device = lax.axis_index("elem")
    rows = []
    for side in range(2):
        ident = neighbours[side]
        place = ident - (device - 1) * width
        here = ident >= 0
        rows.append(jnp.where(here, place % width, 0))
        rows.append(jnp.where(here, place // width, 3))
    for side in range(2, 4):
        ident = neighbours[side]
        here = ident >= 0
        rows.append(jnp.where(here, ident - device * width, 0))
        rows.append(here.astype(jnp.int32))
    return jnp.broadcast_to(jnp.stack(rows)[:, None, :], (8, 8, width))


def inverse_multiplicity(neighbours):
    here = (neighbours >= 0).astype(F32)
    place = jnp.arange(8)
    column = (
        1.0 + here[0][None, :] * (place == 0)[:, None] + here[1][None, :] * (place == 7)[:, None]
    )
    row = 1.0 + here[2][None, :] * (place == 0)[:, None] + here[3][None, :] * (place == 7)[:, None]
    return (1.0 / (row[:, None, :] * column[None, :, :])).reshape(64, -1)


def swap_edges(edges):
    count = lax.axis_size("elem")
    west = lax.ppermute(edges, "elem", [(i, i + 1) for i in range(count - 1)])
    east = lax.ppermute(edges, "elem", [(i + 1, i) for i in range(count - 1)])
    return west, east


def gather_sums(sums):
    count = lax.axis_size("elem")
    spread = jnp.broadcast_to(sums[None], (count,) + sums.shape)
    return lax.all_to_all(spread, "elem", split_axis=0, concat_axis=0, tiled=True)


def per_device(velocity, metric, mass, sponge_rate, sponge_mask, neighbours):
    place = lax.axis_index("mode")
    damping = sponge_mask.astype(F32)[None, :] * sponge_rate
    rows = jnp.concatenate([metric, damping[None], jnp.zeros((3, 64, 128), F32)], axis=0)
    rows = lax.dynamic_slice_in_dim(rows, place * 8, 8, axis=2)
    rows = rows.transpose(0, 2, 1).reshape(8, 512)
    wave = (place * 16 + jnp.arange(16)).astype(F32) * (jnp.pi / 256)
    wave = jnp.broadcast_to(wave[:, None], (16, 128))
    rx, ry, sx, sy = metric[0], metric[1], metric[2], metric[3]
    coef = jnp.stack([mass, -mass * rx, -mass * sx, -mass * ry, -mass * sy])
    stiff = jnp.stack(
        [
            mass * (rx * rx + ry * ry),
            mass * (rx * sx + ry * sy),
            mass * (sx * sx + sy * sy),
            mass,
            inverse_multiplicity(neighbours),
        ]
    )
    links = link_tables(neighbours, 128)
    left = [jnp.asarray(t) for t in left_tables()]

    blocks = to_blocks(velocity)
    blocks = lax.all_to_all(blocks, "mode", split_axis=0, concat_axis=0, tiled=True)
    blocks = in_planes(blocks, rows)
    blocks = lax.all_to_all(blocks, "mode", split_axis=0, concat_axis=0, tiled=True)
    nonlinear, raw, edges = from_blocks(blocks, wave, coef, left[0])
    west, east = swap_edges(edges)
    field, image, edges, sums = image_of(raw, west, east, links, wave, stiff, left, True)
    sums = gather_sums(sums)
    west, east = swap_edges(edges)
    shared, second = image_of(image, west, east, links, wave, stiff, left, False)
    later = gather_sums(residual_sums(field, image, shared, second, sums, stiff))
    return nonlinear, final(field, shared, sums, later)


def solution(mesh):
    return jax.shard_map(
        per_device,
        mesh=mesh,
        in_specs=(
            P(None, None, "mode", None, "elem"),
            P(None, None, "elem"),
            P(None, "elem"),
            P(None, "elem"),
            P("elem"),
            P(None, "elem"),
        ),
        out_specs=(P(None, None, "mode", None, "elem"), P(None, "mode", None, "elem")),
        check_vma=False,
    )
```

```python
import jax
import jax.numpy as jnp
import ml_dtypes
import numpy as np
from jax import lax
from jax.experimental import pallas as pl
from jax.experimental.pallas import tpu as pltpu
from jax.sharding import PartitionSpec as P

F32 = jnp.float32
BF16 = jnp.bfloat16
MIB = 1024 * 1024
WIDE = 48 * MIB
NARROW = 16 * MIB


def cheb_matrix():
    count = 8
    places = np.arange(count)
    points = np.cos(np.pi * places / (count - 1))
    weights = np.where((places == 0) | (places == count - 1), 2.0, 1.0)
    signs = weights * (-1.0) ** places
    differ = points[:, None] - points[None, :] + np.eye(count)
    table = np.outer(signs, 1.0 / signs) / differ
    table = table - np.eye(count) * np.sum(table, axis=1)[:, None]
    return table.astype(np.float32).astype(np.float64)


def two_parts(table):
    high = table.astype(np.float32).astype(ml_dtypes.bfloat16)
    low = (table - high.astype(np.float64)).astype(np.float32).astype(ml_dtypes.bfloat16)
    return high, low


def tables(modes):
    planes = 2 * modes
    order = np.arange(modes)
    spots = np.arange(modes)
    phase = (spots[:, None] * order[None, :]) % planes
    angle = phase * (2.0 * np.pi / planes)
    weight = np.where(order == 0, 1.0, 2.0)
    cosine = np.cos(angle)
    sine = np.sin(angle)
    last = np.zeros((16, modes))
    last[0] = weight * (-1.0) ** order
    synth_cos = np.concatenate([weight * cosine, last], axis=0)
    synth_sin = weight * sine
    back_cos = cosine.T / planes
    back_sin = -sine.T / planes
    wave = np.broadcast_to((order * np.pi / modes)[:, None], (modes, 128)).astype(np.float32)
    sign = np.broadcast_to(((-1.0) ** order / planes)[:, None], (modes, 128)).astype(np.float32)
    return synth_cos, synth_sin, back_cos, back_sin, wave, sign


def right_tables():
    table = cheb_matrix()
    two = np.eye(2)
    eight = np.eye(8)
    along_r = np.kron(two, np.kron(eight, table.T))
    along_s = np.kron(two, np.kron(table.T, eight))
    high, low = two_parts(np.concatenate([along_r, along_s], axis=1))
    return np.concatenate([high, high, low], axis=0)


def left_tables():
    table = cheb_matrix()
    eight = np.eye(8)
    along_r = np.kron(eight, table)
    along_s = np.kron(table, eight)
    high, low = two_parts(np.concatenate([along_r, along_s], axis=0))
    forward = np.concatenate([high, high, low], axis=1)
    high, low = two_parts(np.concatenate([along_r.T, along_s.T], axis=1))
    return forward, np.concatenate([high, high], axis=1), low


def split(value):
    high = value.astype(BF16)
    low = (value - high.astype(F32)).astype(BF16)
    return high, low


def dot(first, second):
    return jnp.dot(first, second, preferred_element_type=F32)


def low_half(shape):
    return lax.broadcasted_iota(jnp.int32, shape, len(shape) - 1) < 64


def swap(value):
    return pltpu.roll(value, 64, 1)


def pre_kernel(v_ref, y_ref, tmp):
    for kl in range(16):
        block = v_ref[0, :, kl].reshape(128, 128)
        tmp[pl.ds(kl, 128, stride=16), :] = block.T
    half = low_half((16, 128))
    for pair in range(64):
        first = tmp[32 * pair : 32 * pair + 16, :]
        second = tmp[32 * pair + 16 : 32 * pair + 32, :]
        g, i = divmod(pair, 4)
        cols = slice(128 * i, 128 * i + 128)
        y_ref[g, 0, 0, :, cols] = jnp.where(half, first, swap(second))
        y_ref[g, 0, 1, :, cols] = jnp.where(half, swap(first), second)


def to_blocks(velocity):
    return pl.pallas_call(
        pre_kernel,
        grid=(3,),
        in_specs=[pl.BlockSpec((1, 2, 16, 64, 128), lambda c: (c, 0, 0, 0, 0))],
        out_specs=pl.BlockSpec((16, 1, 2, 16, 512), lambda c: (0, c, 0, 0, 0)),
        out_shape=jax.ShapeDtypeStruct((16, 3, 2, 16, 512), F32),
        scratch_shapes=[pltpu.VMEM((2048, 128), F32)],
        compiler_params=pltpu.CompilerParams(vmem_limit_bytes=WIDE),
        name="to_blocks",
    )(velocity)


ROWS = 32


def plane_kernel(
    z_ref, rows_ref, wave_ref, sign_ref, slope_ref, cos_ref, sin_ref, back_cos_ref, back_sin_ref, out_ref, high, low, planes, eh, el, tail,
):
    rx = rows_ref[0:1, :]
    ry = rows_ref[1:2, :]
    sx = rows_ref[2:3, :]
    sy = rows_ref[3:4, :]
    damping = rows_ref[4:5, :]
    count = ROWS // 16

    def curls(step, carry):
        rows = pl.ds(pl.multiple_of(step * ROWS, ROWS), ROWS)
        wave = jnp.concatenate([wave_ref[rows, :]] * 2, axis=1)
        fields = {}
        slopes = {}
        for c in range(3):
            for part in range(2):
                value = z_ref[pl.ds(step * count, count), c, part].reshape(ROWS, 256)
                up, down = split(value)
                high[c, part, rows, :] = up
                low[c, part, rows, :] = down
                fields[c, part] = value
                pieces = []
                for q in range(2):
                    cols = slice(128 * q, 128 * q + 128)
                    three = jnp.concatenate([up[:, cols], down[:, cols], up[:, cols]], axis=1)
                    pieces.append(dot(three, slope_ref[...]))
                slopes[c, part] = (
                    jnp.concatenate([pieces[0][:, :128], pieces[1][:, :128]], axis=1),
                    jnp.concatenate([pieces[0][:, 128:], pieces[1][:, 128:]], axis=1),
                )
        for part in range(2):
            u_r, u_s = slopes[0, part]
            v_r, v_s = slopes[1, part]
            w_r, w_s = slopes[2, part]
            if part == 0:
                dz_u = -wave * fields[0, 1]
                dz_v = -wave * fields[1, 1]
            else:
                dz_u = wave * fields[0, 0]
                dz_v = wave * fields[1, 0]
            swirl = (
                ry * w_r + sy * w_s - dz_v,
                dz_u - (rx * w_r + sx * w_s),
                rx * v_r + sx * v_s - (ry * u_r + sy * u_s),
            )
            for c in range(3):
                up, down = split(swirl[c])
                high[3 + c, part, rows, :] = up
                low[3 + c, part, rows, :] = down
        return carry

    lax.fori_loop(0, 256 // ROWS, curls, 0, unroll=True)

    def synth(c, carry):
        even = dot(cos_ref[...], jnp.concatenate([high[c, 0], low[c, 0], high[c, 0]], axis=0))
        odd = dot(sin_ref[...], jnp.concatenate([high[c, 1], low[c, 1], high[c, 1]], axis=0))
        planes[c, 0] = even[:256] - odd
        planes[c, 1] = even[:256] + odd
        planes[c, 1, 0:1, :] = even[256:257, :]
        return carry

    lax.fori_loop(0, 6, synth, 0, unroll=True)

    def force(u, w):
        return (
            u[1] * w[2] - u[2] * w[1] - damping * (u[0] - 1.0),
            u[2] * w[0] - u[0] * w[2] - damping * u[1],
            u[0] * w[1] - u[1] * w[0] - damping * u[2],
        )

    def forces(step, carry):
        rows = pl.ds(pl.multiple_of(step * ROWS, ROWS), ROWS)
        front = [planes[c, 0, rows, :] for c in range(6)]
        back = [planes[c, 1, rows, :] for c in range(6)]
        front = force(front[:3], front[3:])
        back = force(back[:3], back[3:])
        place = lax.broadcasted_iota(jnp.int32, (ROWS, 256), 0) + step * ROWS
        for c in range(3):
            kept = jnp.where(place == 0, 0.0, back[c])
            up, down = split(front[c] + kept)
            eh[c, 0, rows, :] = up
            el[c, 0, rows, :] = down
            up, down = split(front[c] - kept)
            eh[c, 1, rows, :] = up
            el[c, 1, rows, :] = down

        @pl.when(step == 0)
        def _():
            for c in range(3):
                tail[c, 0:8, :] = back[c][0:8, :]

        return carry

    lax.fori_loop(0, 256 // ROWS, forces, 0, unroll=True)

    def analyse(c, carry):
        re = dot(back_cos_ref[...], jnp.concatenate([eh[c, 0], el[c, 0], eh[c, 0]], axis=0))
        im = dot(back_sin_ref[...], jnp.concatenate([eh[c, 1], el[c, 1], eh[c, 1]], axis=0))
        sign = jnp.concatenate([sign_ref[...]] * 2, axis=1)
        re = re + sign * tail[c, 0:1, :]
        out_ref[:, c, 0] = re.reshape(16, 16, 256)
        out_ref[:, c, 1] = im.reshape(16, 16, 256)
        return carry

    lax.fori_loop(0, 3, analyse, 0, unroll=True)


def in_planes(blocks, rows):
    synth_cos, synth_sin, back_cos, back_sin, wave, sign = tables(256)
    consts = [wave, sign, right_tables()]
    for table in (synth_cos, synth_sin, back_cos, back_sin):
        high, low = two_parts(table)
        consts.append(np.concatenate([high, high, low], axis=1))
    consts = [jnp.asarray(c) for c in consts]

    def whole(array):
        return pl.BlockSpec(array.shape, lambda i: (0,) * array.ndim)

    block = pl.BlockSpec((16, 3, 2, 16, 256), lambda i: (0, 0, 0, 0, i))
    return pl.pallas_call(
        plane_kernel,
        grid=(2,),
        in_specs=[block, pl.BlockSpec((8, 256), lambda i: (0, i))] + [whole(c) for c in consts],
        out_specs=block,
        out_shape=jax.ShapeDtypeStruct((16, 3, 2, 16, 512), F32),
        scratch_shapes=[
            pltpu.VMEM((6, 2, 256, 256), BF16),
            pltpu.VMEM((6, 2, 256, 256), BF16),
            pltpu.VMEM((6, 2, 256, 256), F32),
            pltpu.VMEM((3, 2, 256, 256), BF16),
            pltpu.VMEM((3, 2, 256, 256), BF16),
            pltpu.VMEM((3, 8, 256), F32),
        ],
        compiler_params=pltpu.CompilerParams(vmem_limit_bytes=WIDE),
        name="in_planes",
    )(blocks, rows, *consts)


def slopes_of(pair, forward):
    up, down = split(pair)
    both = dot(forward, jnp.concatenate([up, down, up], axis=0))
    return both[:64], both[64:]


def twice(value):
    return jnp.concatenate([value, value], axis=1)


FIELD = (2, 16, 64, 128)
EDGE = (2, 2, 16, 8, 128)


def whole_spec(shape):
    return pl.BlockSpec(shape, lambda i: (0,) * len(shape))


def in_smem():
    return pl.BlockSpec(memory_space=pltpu.SMEM)


def wave_of(ids_ref, kl):
    return (ids_ref[1] * 16 + kl).astype(F32) * (np.pi / 256)


def post_kernel(ids_ref, r_ref, metric_ref, mass_ref, fwd_ref, non_ref, raw_ref, edge_ref, tmp, coef):
    half = low_half((8, 128))
    for c in range(3):
        for pair in range(64):
            g, i = divmod(pair, 4)
            cols = slice(128 * i, 128 * i + 128)
            re = r_ref[g, c, 0, :, cols]
            im = r_ref[g, c, 1, :, cols]
            tmp[c, 16 * pair : 16 * pair + 8, :] = jnp.where(half, re, swap(im))
            tmp[c, 16 * pair + 8 : 16 * pair + 16, :] = jnp.where(half, swap(re), im)
    mass = mass_ref[...]
    coef[0] = -mass * metric_ref[0]
    coef[1] = -mass * metric_ref[2]
    coef[2] = -mass * metric_ref[1]
    coef[3] = -mass * metric_ref[3]
    base = pl.program_id(0) * 8
    for kl in range(8):
        cells = []
        for c in range(3):
            block = tmp[c, pl.ds(kl, 128, stride=8), :].T
            non_ref[c, :, kl] = block.reshape(2, 64, 128)
            cells.append(block)
        x_r, x_s = slopes_of(jnp.concatenate([cells[0][:64], cells[0][64:]], axis=1), fwd_ref[...])
        y_r, y_s = slopes_of(jnp.concatenate([cells[1][:64], cells[1][64:]], axis=1), fwd_ref[...])
        scaled = wave_of(ids_ref, base + kl) * mass_ref[...]
        for part in range(2):
            cols = slice(128 * part, 128 * part + 128)
            value = (
                coef[0] * x_r[:, cols]
                + coef[1] * x_s[:, cols]
                + coef[2] * y_r[:, cols]
                + coef[3] * y_s[:, cols]
            )
            if part == 0:
                value = value + scaled * cells[2][64:]
            else:
                value = value - scaled * cells[2][:64]
            raw_ref[part, kl] = value
            edge_ref[0, part, kl] = raw_ref[part, kl, pl.ds(0, 8, stride=8), :]
            edge_ref[1, part, kl] = raw_ref[part, kl, pl.ds(7, 8, stride=8), :]


def from_blocks(ids, blocks, metric, mass, forward):
    return pl.pallas_call(
        post_kernel,
        grid=(2,),
        in_specs=[
            in_smem(),
            pl.BlockSpec((16, 3, 2, 8, 512), lambda i: (0, 0, 0, i, 0)),
            whole_spec(metric.shape),
            whole_spec(mass.shape),
            whole_spec(forward.shape),
        ],
        out_specs=[
            pl.BlockSpec((3, 2, 8, 64, 128), lambda i: (0, 0, i, 0, 0)),
            pl.BlockSpec((2, 8, 64, 128), lambda i: (0, i, 0, 0)),
            pl.BlockSpec((2, 2, 8, 8, 128), lambda i: (0, 0, i, 0, 0)),
        ],
        out_shape=[
            jax.ShapeDtypeStruct((3, 2, 16, 64, 128), F32),
            jax.ShapeDtypeStruct(FIELD, F32),
            jax.ShapeDtypeStruct(EDGE, F32),
        ],
        scratch_shapes=[pltpu.VMEM((3, 1024, 128), F32), pltpu.VMEM((4, 64, 128), F32)],
        compiler_params=pltpu.CompilerParams(vmem_limit_bytes=NARROW),
        name="from_blocks",
    )(ids, blocks, metric, mass, forward)


def lanes(value, index):
    return jnp.take_along_axis(value, index, axis=1, mode="promise_in_bounds")


def links_of(ids_ref, near_ref):
    device = ids_ref[0]
    links = []
    for side in range(4):
        ident = jnp.broadcast_to(near_ref[side : side + 1, :], (8, 128))
        here = ident >= 0
        if side < 2:
            place = ident - (device - 1) * 128
            links.append((jnp.where(here, place & 127, 0), jnp.where(here, place >> 7, 3)))
        else:
            links.append((jnp.where(here, ident - device * 128, 0), here))
    return links


def share(out_ref, field_ref, west_ref, east_ref, links, part, kl):
    (west_lane, west_from), (east_lane, east_from), (south_lane, south_here), (north_lane, north_here) = links
    first = field_ref[part, kl, pl.ds(0, 8, stride=8), :]
    last = field_ref[part, kl, pl.ds(7, 8, stride=8), :]

    def pick(side, own, lane, origin):
        value = jnp.where(origin == 1, lanes(own, lane), 0.0)
        value = jnp.where(origin == 0, lanes(west_ref[side, part, kl], lane), value)
        return jnp.where(origin == 2, lanes(east_ref[side, part, kl], lane), value)

    out_ref[part, kl] = field_ref[part, kl]
    out_ref[part, kl, pl.ds(0, 8, stride=8), :] = first + pick(1, last, west_lane, west_from)
    out_ref[part, kl, pl.ds(7, 8, stride=8), :] = last + pick(0, first, east_lane, east_from)
    bottom = out_ref[part, kl, 0:8, :]
    top = out_ref[part, kl, 56:64, :]
    out_ref[part, kl, 0:8, :] = bottom + jnp.where(south_here, lanes(top, south_lane), 0.0)
    out_ref[part, kl, 56:64, :] = top + jnp.where(north_here, lanes(bottom, north_lane), 0.0)


def set_stiff(stiff, metric_ref, mass_ref):
    mass = mass_ref[...]
    rx, ry, sx, sy = metric_ref[0], metric_ref[1], metric_ref[2], metric_ref[3]
    stiff[0] = mass * (rx * rx + ry * ry)
    stiff[1] = mass * (rx * sx + ry * sy)
    stiff[2] = mass * (sx * sx + sy * sy)


def set_inverse(inverse, near_ref):
    node = lax.broadcasted_iota(jnp.int32, (64, 128), 0)
    here = [near_ref[side : side + 1, :] >= 0 for side in range(4)]
    places = [(node & 7) == 0, (node & 7) == 7, node < 8, node >= 56]
    value = jnp.ones((64, 128), F32)
    for place, there in zip(places, here):
        value = jnp.where(place & there, 0.5 * value, value)
    inverse[...] = value


def stiffness(pair, shift, stiff, mass_ref, fwd_ref, adj_ref, adl_ref):
    along_r, along_s = slopes_of(pair, fwd_ref[...])
    cross = twice(stiff[1])
    back = jnp.concatenate(
        [
            twice(stiff[0]) * along_r + cross * along_s,
            cross * along_r + twice(stiff[2]) * along_s,
        ],
        axis=0,
    )
    up, down = split(back)
    folded = dot(adj_ref[...], jnp.concatenate([up, down], axis=0)) + dot(adl_ref[...], up)
    return folded + shift * twice(mass_ref[...]) * pair


def image_kernel(
    ids_ref, raw_ref, west_ref, east_ref, near_ref, metric_ref, mass_ref, fwd_ref, adj_ref, adl_ref,
    field_ref, image_ref, edge_ref, stiff,
):
    links = links_of(ids_ref, near_ref)
    set_stiff(stiff, metric_ref, mass_ref)
    for kl in range(16):
        for part in range(2):
            share(field_ref, raw_ref, west_ref, east_ref, links, part, kl)
    for kl in range(16):
        pair = jnp.concatenate([field_ref[0, kl], field_ref[1, kl]], axis=1)
        wave = wave_of(ids_ref, kl)
        image = stiffness(pair, wave * wave + 1.0, stiff, mass_ref, fwd_ref, adj_ref, adl_ref)
        for part in range(2):
            image_ref[part, kl] = image[:, 128 * part : 128 * part + 128]
            edge_ref[0, part, kl] = image_ref[part, kl, pl.ds(0, 8, stride=8), :]
            edge_ref[1, part, kl] = image_ref[part, kl, pl.ds(7, 8, stride=8), :]


def image_of(ids, raw, west, east, near, metric, mass, left):
    return pl.pallas_call(
        image_kernel,
        in_specs=[in_smem()] + [pl.BlockSpec(memory_space=pltpu.VMEM)] * 9,
        out_shape=[
            jax.ShapeDtypeStruct(FIELD, F32),
            jax.ShapeDtypeStruct(FIELD, F32),
            jax.ShapeDtypeStruct(EDGE, F32),
        ],
        scratch_shapes=[pltpu.VMEM((3, 64, 128), F32)],
        compiler_params=pltpu.CompilerParams(vmem_limit_bytes=NARROW),
        name="image",
    )(ids, raw, west, east, near, metric, mass, *left)


def folded_rows(value):
    return jnp.sum(value[0] + value[1], axis=0, keepdims=True)


def moments_kernel(
    ids_ref, image_ref, west_ref, east_ref, field_ref, near_ref, metric_ref, mass_ref, fwd_ref, adj_ref,
    adl_ref, shared_ref, sum_ref, stiff, inverse, second, rows, local,
):
    links = links_of(ids_ref, near_ref)
    set_stiff(stiff, metric_ref, mass_ref)
    set_inverse(inverse, near_ref)
    for kl in range(16):
        for part in range(2):
            share(shared_ref, image_ref, west_ref, east_ref, links, part, kl)
    for kl in range(16):
        pair = jnp.concatenate([shared_ref[0, kl], shared_ref[1, kl]], axis=1)
        wave = wave_of(ids_ref, kl)
        image = stiffness(pair, wave * wave + 1.0, stiff, mass_ref, fwd_ref, adj_ref, adl_ref)
        for part in range(2):
            second[part, kl] = image[:, 128 * part : 128 * part + 128]
        weighed = shared_ref[:, kl] * inverse[...]
        rows[0, kl : kl + 1, :] = folded_rows(weighed * field_ref[:, kl])
        rows[1, kl : kl + 1, :] = folded_rows(weighed * shared_ref[:, kl])
    cross = jnp.sum(rows[0], axis=1, keepdims=True)
    square = jnp.sum(rows[1], axis=1, keepdims=True)
    guess = jnp.where(square > 0.0, cross / jnp.where(square > 0.0, square, 1.0), 0.0)
    local[...] = jnp.broadcast_to(guess, (16, 128))
    for kl in range(16):
        step = local[kl : kl + 1, :]
        one = shared_ref[:, kl]
        two = second[:, kl]
        left = field_ref[:, kl] - step * one
        image = image_ref[:, kl] - step * two
        weighed = left * inverse[...]
        rows[0, kl : kl + 1, :] = folded_rows(left * weighed)
        rows[2, kl : kl + 1, :] = folded_rows(one * weighed)
        rows[3, kl : kl + 1, :] = folded_rows(left * image)
        rows[4, kl : kl + 1, :] = folded_rows(left * two + one * image)
        rows[5, kl : kl + 1, :] = folded_rows(one * two)
    place = lax.broadcasted_iota(jnp.int32, (16, 128), 1)
    packed = local[...]
    for q, row in enumerate((0, 2, 1, 3, 4, 5)):
        packed = jnp.where(place == q + 1, jnp.sum(rows[row], axis=1, keepdims=True), packed)
    for d in range(8):
        sum_ref[d] = packed


def moments_of(ids, image, west, east, field, near, metric, mass, left):
    return pl.pallas_call(
        moments_kernel,
        in_specs=[in_smem()] + [pl.BlockSpec(memory_space=pltpu.VMEM)] * 10,
        out_shape=[jax.ShapeDtypeStruct(FIELD, F32), jax.ShapeDtypeStruct((8, 16, 128), F32)],
        scratch_shapes=[
            pltpu.VMEM((3, 64, 128), F32),
            pltpu.VMEM((64, 128), F32),
            pltpu.VMEM(FIELD, F32),
            pltpu.VMEM((6, 16, 128), F32),
            pltpu.VMEM((16, 128), F32),
        ],
        compiler_params=pltpu.CompilerParams(vmem_limit_bytes=NARROW),
        name="moments",
    )(ids, image, west, east, field, near, metric, mass, *left)


def final_kernel(field_ref, shared_ref, sum_ref, out_ref, scales):
    packed = sum_ref[...]
    place = lax.broadcasted_iota(jnp.int32, packed.shape, 2)
    guess, left2, cross, square, energy, mixed, second = [
        jnp.broadcast_to(
            jnp.sum(jnp.where(place == q, packed, 0.0), axis=2, keepdims=True), packed.shape
        )
        for q in range(7)
    ]
    norm0 = jnp.sum(left2 + guess * (2.0 * cross + guess * square), axis=0)
    energy0 = jnp.sum(cross + guess * square, axis=0)
    alpha0 = norm0 / energy0
    off = guess - alpha0[None]
    norm1 = jnp.sum(left2 + off * (2.0 * cross + off * square), axis=0)
    energy1 = jnp.sum(energy + off * (mixed + off * second), axis=0)
    beta = norm1 / norm0
    alpha1 = norm1 / (energy1 - beta * norm1 / alpha0)
    scales[0] = alpha0 + alpha1 * (1.0 + beta)
    scales[1] = -alpha1 * alpha0
    for kl in range(16):
        one = scales[0, kl : kl + 1, :]
        two = scales[1, kl : kl + 1, :]
        out_ref[:, kl] = one * field_ref[:, kl] + two * shared_ref[:, kl]


def final(field, shared, sums):
    return pl.pallas_call(
        final_kernel,
        out_shape=jax.ShapeDtypeStruct(FIELD, F32),
        scratch_shapes=[pltpu.VMEM((2, 16, 128), F32)],
        compiler_params=pltpu.CompilerParams(vmem_limit_bytes=NARROW),
        name="pressure",
    )(field, shared, sums)


def swap_edges(edges):
    count = lax.axis_size("elem")
    west = lax.ppermute(edges, "elem", [(i, i + 1) for i in range(count - 1)])
    east = lax.ppermute(edges, "elem", [(i + 1, i) for i in range(count - 1)])
    return west, east


def over(array, axis):
    return lax.all_to_all(array, axis, split_axis=0, concat_axis=0, tiled=True)


def per_device(velocity, metric, mass, sponge_rate, sponge_mask, neighbours):
    place = lax.axis_index("mode")
    ids = jnp.stack([lax.axis_index("elem"), place]).astype(jnp.int32)
    damping = sponge_mask.astype(F32)[None, :] * sponge_rate
    rows = jnp.concatenate([metric, damping[None], jnp.zeros((3, 64, 128), F32)], axis=0)
    rows = lax.dynamic_slice_in_dim(rows, place * 8, 8, axis=2)
    rows = rows.transpose(0, 2, 1).reshape(8, 512)
    left = [jnp.asarray(t) for t in left_tables()]

    blocks = over(to_blocks(velocity), "mode")
    blocks = over(in_planes(blocks, rows), "mode")
    nonlinear, raw, edges = from_blocks(ids, blocks, metric, mass, left[0])
    west, east = swap_edges(edges)
    field, image, edges = image_of(ids, raw, west, east, neighbours, metric, mass, left)
    west, east = swap_edges(edges)
    shared, sums = moments_of(ids, image, west, east, field, neighbours, metric, mass, left)
    return nonlinear, final(field, shared, over(sums, "elem"))


def solution(mesh):
    return jax.shard_map(
        per_device,
        mesh=mesh,
        in_specs=(
            P(None, None, "mode", None, "elem"),
            P(None, None, "elem"),
            P(None, "elem"),
            P(None, "elem"),
            P("elem"),
            P(None, "elem"),
        ),
        out_specs=(P(None, None, "mode", None, "elem"), P(None, "mode", None, "elem")),
        check_vma=False,
    )
```

```python
import jax
import jax.numpy as jnp
import ml_dtypes
import numpy as np
from jax import lax
from jax.experimental import pallas as pl
from jax.experimental.pallas import tpu as pltpu
from jax.sharding import PartitionSpec as P

F32 = jnp.float32
BF16 = jnp.bfloat16
MIB = 1024 * 1024
WIDE = 48 * MIB
NARROW = 16 * MIB


def cheb_matrix():
    count = 8
    places = np.arange(count)
    points = np.cos(np.pi * places / (count - 1))
    weights = np.where((places == 0) | (places == count - 1), 2.0, 1.0)
    signs = weights * (-1.0) ** places
    differ = points[:, None] - points[None, :] + np.eye(count)
    table = np.outer(signs, 1.0 / signs) / differ
    table = table - np.eye(count) * np.sum(table, axis=1)[:, None]
    return table.astype(np.float32).astype(np.float64)


def two_parts(table):
    high = table.astype(np.float32).astype(ml_dtypes.bfloat16)
    low = (table - high.astype(np.float64)).astype(np.float32).astype(ml_dtypes.bfloat16)
    return high, low


def tables(modes):
    planes = 2 * modes
    order = np.arange(modes)
    spots = np.arange(modes)
    phase = (spots[:, None] * order[None, :]) % planes
    angle = phase * (2.0 * np.pi / planes)
    weight = np.where(order == 0, 1.0, 2.0)
    cosine = np.cos(angle)
    sine = np.sin(angle)
    last = np.zeros((16, modes))
    last[0] = weight * (-1.0) ** order
    synth_cos = np.concatenate([weight * cosine, last], axis=0)
    synth_sin = weight * sine
    back_cos = cosine.T / planes
    back_sin = -sine.T / planes
    wave = np.broadcast_to((order * np.pi / modes)[:, None], (modes, 128)).astype(np.float32)
    sign = np.broadcast_to(((-1.0) ** order / planes)[:, None], (modes, 128)).astype(np.float32)
    return synth_cos, synth_sin, back_cos, back_sin, wave, sign


def right_tables():
    table = cheb_matrix()
    two = np.eye(2)
    eight = np.eye(8)
    along_r = np.kron(two, np.kron(eight, table.T))
    along_s = np.kron(two, np.kron(table.T, eight))
    high, low = two_parts(np.concatenate([along_r, along_s], axis=1))
    return np.concatenate([high, high, low], axis=0)


def left_tables():
    table = cheb_matrix()
    eight = np.eye(8)
    along_r = np.kron(eight, table)
    along_s = np.kron(table, eight)
    high, low = two_parts(np.concatenate([along_r, along_s], axis=0))
    forward = np.concatenate([high, high, low], axis=1)
    high, low = two_parts(np.concatenate([along_r.T, along_s.T], axis=1))
    return forward, np.concatenate([high, high], axis=1), low


def split(value):
    high = value.astype(BF16)
    low = (value - high.astype(F32)).astype(BF16)
    return high, low


def dot(first, second):
    return jnp.dot(first, second, preferred_element_type=F32)


def low_half(shape):
    return lax.broadcasted_iota(jnp.int32, shape, len(shape) - 1) < 64


def swap(value):
    return pltpu.roll(value, 64, 1)


def pre_kernel(v_ref, y_ref, tmp):
    for kl in range(16):
        block = v_ref[0, :, kl].reshape(128, 128)
        tmp[pl.ds(kl, 128, stride=16), :] = block.T
    half = low_half((16, 128))
    for pair in range(64):
        first = tmp[32 * pair : 32 * pair + 16, :]
        second = tmp[32 * pair + 16 : 32 * pair + 32, :]
        g, i = divmod(pair, 4)
        cols = slice(128 * i, 128 * i + 128)
        y_ref[g, 0, 0, :, cols] = jnp.where(half, first, swap(second))
        y_ref[g, 0, 1, :, cols] = jnp.where(half, swap(first), second)


def to_blocks(velocity):
    return pl.pallas_call(
        pre_kernel,
        grid=(3,),
        in_specs=[pl.BlockSpec((1, 2, 16, 64, 128), lambda c: (c, 0, 0, 0, 0))],
        out_specs=pl.BlockSpec((16, 1, 2, 16, 512), lambda c: (0, c, 0, 0, 0)),
        out_shape=jax.ShapeDtypeStruct((16, 3, 2, 16, 512), F32),
        scratch_shapes=[pltpu.VMEM((2048, 128), F32)],
        compiler_params=pltpu.CompilerParams(vmem_limit_bytes=WIDE),
        name="to_blocks",
    )(velocity)


ROWS = 32


def node_rows(rows, tmp, metric_ref, rate_ref, mask_ref):
    place = pl.multiple_of(lax.axis_index("mode") * 8, 8)
    damping = mask_ref[...].astype(F32) * rate_ref[...]
    blank = jnp.zeros((64, 128), F32)
    for q, value in enumerate([metric_ref[0], metric_ref[1], metric_ref[2], metric_ref[3], damping]):
        tmp[q] = jnp.concatenate([value, blank], axis=0).T
    for q in range(5):
        mine = tmp[q, pl.ds(place, 8), :]
        other = swap(mine)
        for i in range(4):
            row = mine[2 * i : 2 * i + 1, :] + other[2 * i + 1 : 2 * i + 2, :]
            rows[i // 2, q : q + 1, 128 * (i % 2) : 128 * (i % 2) + 128] = row


def plane_kernel(
    z_ref, metric_ref, rate_ref, mask_ref, wave_ref, sign_ref, slope_ref, cos_ref, sin_ref,
    back_cos_ref, back_sin_ref, out_ref, high, low, planes, eh, el, tail, grads, rows_all, turned,
):
    @pl.when(pl.program_id(0) == 0)
    def _():
        node_rows(rows_all, turned, metric_ref, rate_ref, mask_ref)

    node = rows_all[pl.program_id(0)]
    rx = node[0:1, :]
    ry = node[1:2, :]
    sx = node[2:3, :]
    sy = node[3:4, :]
    damping = node[4:5, :]
    count = ROWS // 16

    for c in range(3):
        for part in range(2):
            up, down = split(z_ref[:, c, part].reshape(256, 256))
            high[c, part] = up
            low[c, part] = down
            for q in range(2):
                cols = slice(128 * q, 128 * q + 128)
                three = jnp.concatenate([up[:, cols], down[:, cols], up[:, cols]], axis=1)
                both = dot(three, slope_ref[...])
                grads[c, part, 0, :, cols] = both[:, :128]
                grads[c, part, 1, :, cols] = both[:, 128:]

    def curls(step, carry):
        rows = pl.ds(pl.multiple_of(step * ROWS, ROWS), ROWS)
        wave = jnp.concatenate([wave_ref[rows, :]] * 2, axis=1)
        for part in range(2):
            u_r, u_s = grads[0, part, 0, rows, :], grads[0, part, 1, rows, :]
            v_r, v_s = grads[1, part, 0, rows, :], grads[1, part, 1, rows, :]
            w_r, w_s = grads[2, part, 0, rows, :], grads[2, part, 1, rows, :]
            u_t = z_ref[pl.ds(step * count, count), 0, 1 - part].reshape(ROWS, 256)
            v_t = z_ref[pl.ds(step * count, count), 1, 1 - part].reshape(ROWS, 256)
            turn = -wave if part == 0 else wave
            swirl = (
                ry * w_r + sy * w_s - turn * v_t,
                turn * u_t - (rx * w_r + sx * w_s),
                rx * v_r + sx * v_s - (ry * u_r + sy * u_s),
            )
            for c in range(3):
                up, down = split(swirl[c])
                high[3 + c, part, rows, :] = up
                low[3 + c, part, rows, :] = down
        return carry

    lax.fori_loop(0, 256 // ROWS, curls, 0, unroll=True)

    def synth(c, carry):
        even = dot(cos_ref[...], jnp.concatenate([high[c, 0], low[c, 0], high[c, 0]], axis=0))
        odd = dot(sin_ref[...], jnp.concatenate([high[c, 1], low[c, 1], high[c, 1]], axis=0))
        planes[c, 0] = even[:256] - odd
        planes[c, 1] = even[:256] + odd
        planes[c, 1, 0:1, :] = even[256:257, :]
        return carry

    lax.fori_loop(0, 6, synth, 0, unroll=True)

    def force(u, w):
        return (
            u[1] * w[2] - u[2] * w[1] - damping * (u[0] - 1.0),
            u[2] * w[0] - u[0] * w[2] - damping * u[1],
            u[0] * w[1] - u[1] * w[0] - damping * u[2],
        )

    def forces(step, carry):
        rows = pl.ds(pl.multiple_of(step * ROWS, ROWS), ROWS)
        front = [planes[c, 0, rows, :] for c in range(6)]
        back = [planes[c, 1, rows, :] for c in range(6)]
        front = force(front[:3], front[3:])
        back = force(back[:3], back[3:])
        place = lax.broadcasted_iota(jnp.int32, (ROWS, 256), 0) + step * ROWS
        for c in range(3):
            kept = jnp.where(place == 0, 0.0, back[c])
            up, down = split(front[c] + kept)
            eh[c, 0, rows, :] = up
            el[c, 0, rows, :] = down
            up, down = split(front[c] - kept)
            eh[c, 1, rows, :] = up
            el[c, 1, rows, :] = down

        @pl.when(step == 0)
        def _():
            for c in range(3):
                tail[c, 0:8, :] = back[c][0:8, :]

        return carry

    lax.fori_loop(0, 256 // ROWS, forces, 0, unroll=True)

    def analyse(c, carry):
        re = dot(back_cos_ref[...], jnp.concatenate([eh[c, 0], el[c, 0], eh[c, 0]], axis=0))
        im = dot(back_sin_ref[...], jnp.concatenate([eh[c, 1], el[c, 1], eh[c, 1]], axis=0))
        sign = jnp.concatenate([sign_ref[...]] * 2, axis=1)
        re = re + sign * tail[c, 0:1, :]
        out_ref[:, c, 0] = re.reshape(16, 16, 256)
        out_ref[:, c, 1] = im.reshape(16, 16, 256)
        return carry

    lax.fori_loop(0, 3, analyse, 0, unroll=True)


def in_planes(blocks, metric, rate, mask):
    synth_cos, synth_sin, back_cos, back_sin, wave, sign = tables(256)
    consts = [wave, sign, right_tables()]
    for table in (synth_cos, synth_sin, back_cos, back_sin):
        high, low = two_parts(table)
        consts.append(np.concatenate([high, high, low], axis=1))
    consts = [jnp.asarray(c) for c in consts]

    def whole(array):
        return pl.BlockSpec(array.shape, lambda i: (0,) * array.ndim)

    block = pl.BlockSpec((16, 3, 2, 16, 256), lambda i: (0, 0, 0, 0, i))
    return pl.pallas_call(
        plane_kernel,
        grid=(2,),
        in_specs=[block] + [whole(c) for c in [metric, rate, mask] + consts],
        out_specs=block,
        out_shape=jax.ShapeDtypeStruct((16, 3, 2, 16, 512), F32),
        scratch_shapes=[
            pltpu.VMEM((6, 2, 256, 256), BF16),
            pltpu.VMEM((6, 2, 256, 256), BF16),
            pltpu.VMEM((6, 2, 256, 256), F32),
            pltpu.VMEM((3, 2, 256, 256), BF16),
            pltpu.VMEM((3, 2, 256, 256), BF16),
            pltpu.VMEM((3, 8, 256), F32),
            pltpu.VMEM((3, 2, 2, 256, 256), F32),
            pltpu.VMEM((2, 8, 256), F32),
            pltpu.VMEM((5, 128, 128), F32),
        ],
        compiler_params=pltpu.CompilerParams(vmem_limit_bytes=WIDE),
        name="in_planes",
    )(blocks, metric, rate, mask, *consts)


def slopes_of(pair, forward):
    up, down = split(pair)
    both = dot(forward, jnp.concatenate([up, down, up], axis=0))
    return both[:64], both[64:]


def twice(value):
    return jnp.concatenate([value, value], axis=1)


FIELD = (2, 16, 64, 128)
EDGE = (2, 2, 16, 8, 128)


def whole_spec(shape):
    return pl.BlockSpec(shape, lambda i: (0,) * len(shape))


def wave_of(kl):
    return (lax.axis_index("mode") * 16 + kl).astype(F32) * (np.pi / 256)


def post_kernel(r_ref, metric_ref, mass_ref, fwd_ref, non_ref, raw_ref, edge_ref, tmp, coef):
    half = low_half((8, 128))
    for c in range(3):
        for pair in range(64):
            g, i = divmod(pair, 4)
            cols = slice(128 * i, 128 * i + 128)
            re = r_ref[g, c, 0, :, cols]
            im = r_ref[g, c, 1, :, cols]
            tmp[c, 16 * pair : 16 * pair + 8, :] = jnp.where(half, re, swap(im))
            tmp[c, 16 * pair + 8 : 16 * pair + 16, :] = jnp.where(half, swap(re), im)
    mass = mass_ref[...]
    coef[0] = -mass * metric_ref[0]
    coef[1] = -mass * metric_ref[2]
    coef[2] = -mass * metric_ref[1]
    coef[3] = -mass * metric_ref[3]
    base = pl.program_id(0) * 8
    for kl in range(8):
        cells = []
        for c in range(3):
            block = tmp[c, pl.ds(kl, 128, stride=8), :].T
            non_ref[c, :, kl] = block.reshape(2, 64, 128)
            cells.append(block)
        x_r, x_s = slopes_of(jnp.concatenate([cells[0][:64], cells[0][64:]], axis=1), fwd_ref[...])
        y_r, y_s = slopes_of(jnp.concatenate([cells[1][:64], cells[1][64:]], axis=1), fwd_ref[...])
        scaled = wave_of(base + kl) * mass_ref[...]
        for part in range(2):
            cols = slice(128 * part, 128 * part + 128)
            value = (
                coef[0] * x_r[:, cols]
                + coef[1] * x_s[:, cols]
                + coef[2] * y_r[:, cols]
                + coef[3] * y_s[:, cols]
            )
            if part == 0:
                value = value + scaled * cells[2][64:]
            else:
                value = value - scaled * cells[2][:64]
            raw_ref[part, kl] = value
            edge_ref[0, part, kl] = raw_ref[part, kl, pl.ds(0, 8, stride=8), :]
            edge_ref[1, part, kl] = raw_ref[part, kl, pl.ds(7, 8, stride=8), :]


def from_blocks(blocks, metric, mass, forward):
    return pl.pallas_call(
        post_kernel,
        grid=(2,),
        in_specs=[
            pl.BlockSpec((16, 3, 2, 8, 512), lambda i: (0, 0, 0, i, 0)),
            whole_spec(metric.shape),
            whole_spec(mass.shape),
            whole_spec(forward.shape),
        ],
        out_specs=[
            pl.BlockSpec((3, 2, 8, 64, 128), lambda i: (0, 0, i, 0, 0)),
            pl.BlockSpec((2, 8, 64, 128), lambda i: (0, i, 0, 0)),
            pl.BlockSpec((2, 2, 8, 8, 128), lambda i: (0, 0, i, 0, 0)),
        ],
        out_shape=[
            jax.ShapeDtypeStruct((3, 2, 16, 64, 128), F32),
            jax.ShapeDtypeStruct(FIELD, F32),
            jax.ShapeDtypeStruct(EDGE, F32),
        ],
        scratch_shapes=[pltpu.VMEM((3, 1024, 128), F32), pltpu.VMEM((4, 64, 128), F32)],
        compiler_params=pltpu.CompilerParams(vmem_limit_bytes=NARROW),
        name="from_blocks",
    )(blocks, metric, mass, forward)


def lanes(value, index):
    return jnp.take_along_axis(value, index, axis=1, mode="promise_in_bounds")


def links_of(link_ref):
    device = lax.axis_index("elem")
    links = []
    for side in range(4):
        ident = jnp.broadcast_to(link_ref[side : side + 1, :], (8, 128))
        here = ident >= 0
        if side < 2:
            place = ident - (device - 1) * 128
            origin = place >> 7
            origin = jnp.where((device & 1) == 1, origin, 2 - origin)
            links.append((jnp.where(here, place & 127, 0), jnp.where(here, origin, 3)))
        else:
            links.append((jnp.where(here, ident - device * 128, 0), here))
    return links


def share(out_ref, field_ref, near_edge, far_edge, links, part, kl):
    (west_lane, west_from), (east_lane, east_from), (south_lane, south_here), (north_lane, north_here) = links
    first = field_ref[part, kl, pl.ds(0, 8, stride=8), :]
    last = field_ref[part, kl, pl.ds(7, 8, stride=8), :]

    def pick(side, own, lane, origin):
        value = jnp.where(origin == 1, lanes(own, lane), 0.0)
        value = jnp.where(origin == 0, lanes(near_edge[side, part, kl], lane), value)
        return jnp.where(origin == 2, lanes(far_edge[side, part, kl], lane), value)

    out_ref[part, kl] = field_ref[part, kl]
    out_ref[part, kl, pl.ds(0, 8, stride=8), :] = first + pick(1, last, west_lane, west_from)
    out_ref[part, kl, pl.ds(7, 8, stride=8), :] = last + pick(0, first, east_lane, east_from)
    bottom = out_ref[part, kl, 0:8, :]
    top = out_ref[part, kl, 56:64, :]
    out_ref[part, kl, 0:8, :] = bottom + jnp.where(south_here, lanes(top, south_lane), 0.0)
    out_ref[part, kl, 56:64, :] = top + jnp.where(north_here, lanes(bottom, north_lane), 0.0)


def set_stiff(stiff, metric_ref, mass_ref):
    mass = mass_ref[...]
    rx, ry, sx, sy = metric_ref[0], metric_ref[1], metric_ref[2], metric_ref[3]
    stiff[0] = mass * (rx * rx + ry * ry)
    stiff[1] = mass * (rx * sx + ry * sy)
    stiff[2] = mass * (sx * sx + sy * sy)


def set_inverse(inverse, link_ref):
    node = lax.broadcasted_iota(jnp.int32, (64, 128), 0)
    here = [link_ref[side : side + 1, :] >= 0 for side in range(4)]
    places = [(node & 7) == 0, (node & 7) == 7, node < 8, node >= 56]
    value = jnp.ones((64, 128), F32)
    for place, there in zip(places, here):
        value = jnp.where(place & there, 0.5 * value, value)
    inverse[...] = value


def stiffness(pair, shift, stiff, mass_ref, fwd_ref, adj_ref, adl_ref):
    along_r, along_s = slopes_of(pair, fwd_ref[...])
    cross = twice(stiff[1])
    back = jnp.concatenate(
        [
            twice(stiff[0]) * along_r + cross * along_s,
            cross * along_r + twice(stiff[2]) * along_s,
        ],
        axis=0,
    )
    up, down = split(back)
    folded = dot(adj_ref[...], jnp.concatenate([up, down], axis=0)) + dot(adl_ref[...], up)
    return folded + shift * twice(mass_ref[...]) * pair


def image_kernel(
    raw_ref, near_edge, far_edge, link_ref, metric_ref, mass_ref, fwd_ref, adj_ref, adl_ref,
    field_ref, image_ref, edge_ref, stiff,
):
    links = links_of(link_ref)
    set_stiff(stiff, metric_ref, mass_ref)
    for kl in range(16):
        for part in range(2):
            share(field_ref, raw_ref, near_edge, far_edge, links, part, kl)
    for kl in range(16):
        pair = jnp.concatenate([field_ref[0, kl], field_ref[1, kl]], axis=1)
        wave = wave_of(kl)
        image = stiffness(pair, wave * wave + 1.0, stiff, mass_ref, fwd_ref, adj_ref, adl_ref)
        for part in range(2):
            image_ref[part, kl] = image[:, 128 * part : 128 * part + 128]
            edge_ref[0, part, kl] = image_ref[part, kl, pl.ds(0, 8, stride=8), :]
            edge_ref[1, part, kl] = image_ref[part, kl, pl.ds(7, 8, stride=8), :]


def image_of(raw, near, far, links, metric, mass, left):
    return pl.pallas_call(
        image_kernel,
        in_specs=[pl.BlockSpec(memory_space=pltpu.VMEM)] * 9,
        out_shape=[
            jax.ShapeDtypeStruct(FIELD, F32),
            jax.ShapeDtypeStruct(FIELD, F32),
            jax.ShapeDtypeStruct(EDGE, F32),
        ],
        scratch_shapes=[pltpu.VMEM((3, 64, 128), F32)],
        compiler_params=pltpu.CompilerParams(vmem_limit_bytes=NARROW),
        name="image",
    )(raw, near, far, links, metric, mass, *left)


def folded_rows(value):
    return jnp.sum(value[0] + value[1], axis=0, keepdims=True)


def moments_kernel(
    image_ref, near_edge, far_edge, field_ref, link_ref, metric_ref, mass_ref, fwd_ref, adj_ref,
    adl_ref, shared_ref, sum_ref, stiff, inverse, second, rows, local,
):
    links = links_of(link_ref)
    set_stiff(stiff, metric_ref, mass_ref)
    set_inverse(inverse, link_ref)
    for kl in range(16):
        for part in range(2):
            share(shared_ref, image_ref, near_edge, far_edge, links, part, kl)
    for kl in range(16):
        pair = jnp.concatenate([shared_ref[0, kl], shared_ref[1, kl]], axis=1)
        wave = wave_of(kl)
        image = stiffness(pair, wave * wave + 1.0, stiff, mass_ref, fwd_ref, adj_ref, adl_ref)
        for part in range(2):
            second[part, kl] = image[:, 128 * part : 128 * part + 128]
        weighed = shared_ref[:, kl] * inverse[...]
        rows[0, kl : kl + 1, :] = folded_rows(weighed * field_ref[:, kl])
        rows[1, kl : kl + 1, :] = folded_rows(weighed * shared_ref[:, kl])
    cross = jnp.sum(rows[0], axis=1, keepdims=True)
    square = jnp.sum(rows[1], axis=1, keepdims=True)
    guess = jnp.where(square > 0.0, cross / jnp.where(square > 0.0, square, 1.0), 0.0)
    local[...] = jnp.broadcast_to(guess, (16, 128))
    for kl in range(16):
        step = local[kl : kl + 1, :]
        one = shared_ref[:, kl]
        two = second[:, kl]
        left = field_ref[:, kl] - step * one
        image = image_ref[:, kl] - step * two
        weighed = left * inverse[...]
        rows[0, kl : kl + 1, :] = folded_rows(left * weighed)
        rows[2, kl : kl + 1, :] = folded_rows(one * weighed)
        rows[3, kl : kl + 1, :] = folded_rows(left * image)
        rows[4, kl : kl + 1, :] = folded_rows(left * two + one * image)
        rows[5, kl : kl + 1, :] = folded_rows(one * two)
    place = lax.broadcasted_iota(jnp.int32, (16, 128), 1)
    packed = local[...]
    for q, row in enumerate((0, 2, 1, 3, 4, 5)):
        packed = jnp.where(place == q + 1, jnp.sum(rows[row], axis=1, keepdims=True), packed)
    for d in range(8):
        sum_ref[d] = packed


def moments_of(image, near, far, field, links, metric, mass, left):
    return pl.pallas_call(
        moments_kernel,
        in_specs=[pl.BlockSpec(memory_space=pltpu.VMEM)] * 10,
        out_shape=[jax.ShapeDtypeStruct(FIELD, F32), jax.ShapeDtypeStruct((8, 16, 128), F32)],
        scratch_shapes=[
            pltpu.VMEM((3, 64, 128), F32),
            pltpu.VMEM((64, 128), F32),
            pltpu.VMEM(FIELD, F32),
            pltpu.VMEM((6, 16, 128), F32),
            pltpu.VMEM((16, 128), F32),
        ],
        compiler_params=pltpu.CompilerParams(vmem_limit_bytes=NARROW),
        name="moments",
    )(image, near, far, field, links, metric, mass, *left)


def final_kernel(field_ref, shared_ref, sum_ref, out_ref, scales):
    packed = sum_ref[...]
    place = lax.broadcasted_iota(jnp.int32, packed.shape, 2)
    guess, left2, cross, square, energy, mixed, second = [
        jnp.broadcast_to(
            jnp.sum(jnp.where(place == q, packed, 0.0), axis=2, keepdims=True), packed.shape
        )
        for q in range(7)
    ]
    norm0 = jnp.sum(left2 + guess * (2.0 * cross + guess * square), axis=0)
    energy0 = jnp.sum(cross + guess * square, axis=0)
    alpha0 = norm0 / energy0
    off = guess - alpha0[None]
    norm1 = jnp.sum(left2 + off * (2.0 * cross + off * square), axis=0)
    energy1 = jnp.sum(energy + off * (mixed + off * second), axis=0)
    beta = norm1 / norm0
    alpha1 = norm1 / (energy1 - beta * norm1 / alpha0)
    scales[0] = alpha0 + alpha1 * (1.0 + beta)
    scales[1] = -alpha1 * alpha0
    for kl in range(16):
        one = scales[0, kl : kl + 1, :]
        two = scales[1, kl : kl + 1, :]
        out_ref[:, kl] = one * field_ref[:, kl] + two * shared_ref[:, kl]


def final(field, shared, sums):
    return pl.pallas_call(
        final_kernel,
        out_shape=jax.ShapeDtypeStruct(FIELD, F32),
        scratch_shapes=[pltpu.VMEM((2, 16, 128), F32)],
        compiler_params=pltpu.CompilerParams(vmem_limit_bytes=NARROW),
        name="pressure",
    )(field, shared, sums)


def swap_edges(edges):
    count = lax.axis_size("elem")
    far = [pair for i in range(1, count - 1, 2) for pair in ((i, i + 1), (i + 1, i))]
    far = lax.ppermute(edges, "elem", far)
    near = lax.ppermute(edges, "elem", [(i, i ^ 1) for i in range(count)])
    return near, far


def over(array, axis):
    return lax.all_to_all(array, axis, split_axis=0, concat_axis=0, tiled=True)


def per_device(velocity, metric, mass, sponge_rate, sponge_mask, neighbours):
    left = [jnp.asarray(t) for t in left_tables()]

    blocks = over(to_blocks(velocity), "mode")
    blocks = in_planes(blocks, metric, sponge_rate, sponge_mask.reshape(1, 128))
    blocks = over(blocks, "mode")
    nonlinear, raw, edges = from_blocks(blocks, metric, mass, left[0])
    near, far = swap_edges(edges)
    field, image, edges = image_of(raw, near, far, neighbours, metric, mass, left)
    near, far = swap_edges(edges)
    shared, sums = moments_of(image, near, far, field, neighbours, metric, mass, left)
    return nonlinear, final(field, shared, over(sums, "elem"))


def solution(mesh):
    return jax.shard_map(
        per_device,
        mesh=mesh,
        in_specs=(
            P(None, None, "mode", None, "elem"),
            P(None, None, "elem"),
            P(None, "elem"),
            P(None, "elem"),
            P("elem"),
            P(None, "elem"),
        ),
        out_specs=(P(None, None, "mode", None, "elem"), P(None, "mode", None, "elem")),
        check_vma=False,
    )
```

```python
import jax
import jax.numpy as jnp
import ml_dtypes
import numpy as np
from jax import lax
from jax.experimental import pallas as pl
from jax.experimental.pallas import tpu as pltpu
from jax.sharding import PartitionSpec as P

F32 = jnp.float32
BF16 = jnp.bfloat16
MIB = 1024 * 1024
WIDE = 48 * MIB
NARROW = 16 * MIB
SMALL = pl.CostEstimate(flops=1000, bytes_accessed=1000, transcendentals=0)


def cheb_matrix():
    count = 8
    places = np.arange(count)
    points = np.cos(np.pi * places / (count - 1))
    weights = np.where((places == 0) | (places == count - 1), 2.0, 1.0)
    signs = weights * (-1.0) ** places
    differ = points[:, None] - points[None, :] + np.eye(count)
    table = np.outer(signs, 1.0 / signs) / differ
    table = table - np.eye(count) * np.sum(table, axis=1)[:, None]
    return table.astype(np.float32).astype(np.float64)


def two_parts(table):
    high = table.astype(np.float32).astype(ml_dtypes.bfloat16)
    low = (table - high.astype(np.float64)).astype(np.float32).astype(ml_dtypes.bfloat16)
    return high, low


def tables(modes):
    planes = 2 * modes
    order = np.arange(modes)
    spots = np.arange(modes)
    phase = (spots[:, None] * order[None, :]) % planes
    angle = phase * (2.0 * np.pi / planes)
    weight = np.where(order == 0, 1.0, 2.0)
    cosine = np.cos(angle)
    sine = np.sin(angle)
    last = np.zeros((16, modes))
    last[0] = weight * (-1.0) ** order
    synth_cos = np.concatenate([weight * cosine, last], axis=0)
    synth_sin = weight * sine
    back_cos = cosine.T / planes
    back_sin = -sine.T / planes
    wave = np.broadcast_to((order * np.pi / modes)[:, None], (modes, 128)).astype(np.float32)
    sign = np.broadcast_to(((-1.0) ** order / planes)[:, None], (modes, 128)).astype(np.float32)
    return synth_cos, synth_sin, back_cos, back_sin, wave, sign


def right_tables():
    table = cheb_matrix()
    two = np.eye(2)
    eight = np.eye(8)
    along_r = np.kron(two, np.kron(eight, table.T))
    along_s = np.kron(two, np.kron(table.T, eight))
    high, low = two_parts(np.concatenate([along_r, along_s], axis=1))
    return np.concatenate([high, high, low], axis=0)


def left_tables():
    table = cheb_matrix()
    eight = np.eye(8)
    along_r = np.kron(eight, table)
    along_s = np.kron(table, eight)
    high, low = two_parts(np.concatenate([along_r, along_s], axis=0))
    forward = np.concatenate([high, high, low], axis=1)
    high, low = two_parts(np.concatenate([along_r.T, along_s.T], axis=1))
    return forward, np.concatenate([high, high], axis=1), low


def split(value):
    high = value.astype(BF16)
    low = (value - high.astype(F32)).astype(BF16)
    return high, low


def dot(first, second):
    return jnp.dot(first, second, preferred_element_type=F32)


def low_half(shape):
    return lax.broadcasted_iota(jnp.int32, shape, len(shape) - 1) < 64


def swap(value):
    return pltpu.roll(value, 64, 1)


def pre_kernel(v_ref, y_ref, tmp):
    for kl in range(16):
        block = v_ref[0, :, kl].reshape(128, 128)
        tmp[pl.ds(kl, 128, stride=16), :] = block.T
    half = low_half((16, 128))
    for pair in range(64):
        first = tmp[32 * pair : 32 * pair + 16, :]
        second = tmp[32 * pair + 16 : 32 * pair + 32, :]
        g, i = divmod(pair, 4)
        cols = slice(128 * i, 128 * i + 128)
        y_ref[g, 0, 0, :, cols] = jnp.where(half, first, swap(second))
        y_ref[g, 0, 1, :, cols] = jnp.where(half, swap(first), second)


def to_blocks(velocity):
    return pl.pallas_call(
        pre_kernel,
        grid=(3,),
        in_specs=[pl.BlockSpec((1, 2, 16, 64, 128), lambda c: (c, 0, 0, 0, 0))],
        out_specs=pl.BlockSpec((16, 1, 2, 16, 512), lambda c: (0, c, 0, 0, 0)),
        out_shape=jax.ShapeDtypeStruct((16, 3, 2, 16, 512), F32),
        scratch_shapes=[pltpu.VMEM((2048, 128), F32)],
        compiler_params=pltpu.CompilerParams(vmem_limit_bytes=WIDE),
        name="to_blocks",
    )(velocity)


ROWS = 32


def node_rows(rows, tmp, metric_ref, rate_ref, mask_ref, mass_ref):
    place = pl.multiple_of(lax.axis_index("mode") * 8, 8)
    damping = mask_ref[...].astype(F32) * rate_ref[...]
    blank = jnp.zeros((64, 128), F32)
    values = [metric_ref[0], metric_ref[1], metric_ref[2], metric_ref[3], damping, mass_ref[...]]
    for q, value in enumerate(values):
        tmp[q] = jnp.concatenate([value, blank], axis=0).T
    for q in range(6):
        mine = tmp[q, pl.ds(place, 8), :]
        other = swap(mine)
        for i in range(4):
            row = mine[2 * i : 2 * i + 1, :] + other[2 * i + 1 : 2 * i + 2, :]
            rows[i // 2, q : q + 1, 128 * (i % 2) : 128 * (i % 2) + 128] = row


def plane_kernel(
    z_ref, metric_ref, rate_ref, mask_ref, mass_ref, wave_ref, sign_ref, slope_ref, cos_ref, sin_ref,
    back_cos_ref, back_sin_ref, out_ref, raw_ref, high, low, planes, eh, el, tail, grads, rows_all, turned,
):
    @pl.when(pl.program_id(0) == 0)
    def _():
        node_rows(rows_all, turned, metric_ref, rate_ref, mask_ref, mass_ref)

    node = rows_all[pl.program_id(0)]
    rx = node[0:1, :]
    ry = node[1:2, :]
    sx = node[2:3, :]
    sy = node[3:4, :]
    damping = node[4:5, :]
    mass = node[5:6, :]
    count = ROWS // 16

    for c in range(3):
        for part in range(2):
            up, down = split(z_ref[:, c, part].reshape(256, 256))
            high[c, part] = up
            low[c, part] = down
            for q in range(2):
                cols = slice(128 * q, 128 * q + 128)
                three = jnp.concatenate([up[:, cols], down[:, cols], up[:, cols]], axis=1)
                both = dot(three, slope_ref[...])
                grads[c, part, 0, :, cols] = both[:, :128]
                grads[c, part, 1, :, cols] = both[:, 128:]

    def curls(step, carry):
        rows = pl.ds(pl.multiple_of(step * ROWS, ROWS), ROWS)
        wave = jnp.concatenate([wave_ref[rows, :]] * 2, axis=1)
        for part in range(2):
            u_r, u_s = grads[0, part, 0, rows, :], grads[0, part, 1, rows, :]
            v_r, v_s = grads[1, part, 0, rows, :], grads[1, part, 1, rows, :]
            w_r, w_s = grads[2, part, 0, rows, :], grads[2, part, 1, rows, :]
            u_t = z_ref[pl.ds(step * count, count), 0, 1 - part].reshape(ROWS, 256)
            v_t = z_ref[pl.ds(step * count, count), 1, 1 - part].reshape(ROWS, 256)
            turn = -wave if part == 0 else wave
            swirl = (
                ry * w_r + sy * w_s - turn * v_t,
                turn * u_t - (rx * w_r + sx * w_s),
                rx * v_r + sx * v_s - (ry * u_r + sy * u_s),
            )
            for c in range(3):
                up, down = split(swirl[c])
                high[3 + c, part, rows, :] = up
                low[3 + c, part, rows, :] = down
        return carry

    lax.fori_loop(0, 256 // ROWS, curls, 0, unroll=True)

    def synth(c, carry):
        even = dot(cos_ref[...], jnp.concatenate([high[c, 0], low[c, 0], high[c, 0]], axis=0))
        odd = dot(sin_ref[...], jnp.concatenate([high[c, 1], low[c, 1], high[c, 1]], axis=0))
        planes[c, 0] = even[:256] - odd
        planes[c, 1] = even[:256] + odd
        planes[c, 1, 0:1, :] = even[256:257, :]
        return carry

    lax.fori_loop(0, 6, synth, 0, unroll=True)

    def force(u, w):
        return (
            u[1] * w[2] - u[2] * w[1] - damping * (u[0] - 1.0),
            u[2] * w[0] - u[0] * w[2] - damping * u[1],
            u[0] * w[1] - u[1] * w[0] - damping * u[2],
        )

    def forces(step, carry):
        rows = pl.ds(pl.multiple_of(step * ROWS, ROWS), ROWS)
        front = [planes[c, 0, rows, :] for c in range(6)]
        back = [planes[c, 1, rows, :] for c in range(6)]
        front = force(front[:3], front[3:])
        back = force(back[:3], back[3:])
        place = lax.broadcasted_iota(jnp.int32, (ROWS, 256), 0) + step * ROWS
        for c in range(3):
            kept = jnp.where(place == 0, 0.0, back[c])
            up, down = split(front[c] + kept)
            eh[c, 0, rows, :] = up
            el[c, 0, rows, :] = down
            up, down = split(front[c] - kept)
            eh[c, 1, rows, :] = up
            el[c, 1, rows, :] = down

        @pl.when(step == 0)
        def _():
            for c in range(3):
                tail[c, 0:8, :] = back[c][0:8, :]

        return carry

    lax.fori_loop(0, 256 // ROWS, forces, 0, unroll=True)

    def analyse(c, carry):
        re = dot(back_cos_ref[...], jnp.concatenate([eh[c, 0], el[c, 0], eh[c, 0]], axis=0))
        im = dot(back_sin_ref[...], jnp.concatenate([eh[c, 1], el[c, 1], eh[c, 1]], axis=0))
        sign = jnp.concatenate([sign_ref[...]] * 2, axis=1)
        re = re + sign * tail[c, 0:1, :]
        out_ref[:, c, 0] = re.reshape(16, 16, 256)
        out_ref[:, c, 1] = im.reshape(16, 16, 256)
        return carry

    lax.fori_loop(0, 3, analyse, 0, unroll=True)

    for c in range(2):
        for part in range(2):
            up, down = split(out_ref[:, c, part].reshape(256, 256))
            for q in range(2):
                cols = slice(128 * q, 128 * q + 128)
                three = jnp.concatenate([up[:, cols], down[:, cols], up[:, cols]], axis=1)
                both = dot(three, slope_ref[...])
                grads[c, part, 0, :, cols] = both[:, :128]
                grads[c, part, 1, :, cols] = both[:, 128:]
    x_r, x_s, y_r, y_s = -mass * rx, -mass * sx, -mass * ry, -mass * sy
    for step in range(256 // ROWS):
        rows = slice(step * ROWS, step * ROWS + ROWS)
        wave = jnp.concatenate([wave_ref[rows, :]] * 2, axis=1)
        for part in range(2):
            other = out_ref[count * step : count * step + count, 2, 1 - part].reshape(ROWS, 256)
            turn = wave if part == 0 else -wave
            value = (
                x_r * grads[0, part, 0, rows, :]
                + x_s * grads[0, part, 1, rows, :]
                + y_r * grads[1, part, 0, rows, :]
                + y_s * grads[1, part, 1, rows, :]
                + mass * (turn * other)
            )
            raw_ref[count * step : count * step + count, part] = value.reshape(count, 16, 256)


def in_planes(blocks, metric, rate, mask, mass):
    synth_cos, synth_sin, back_cos, back_sin, wave, sign = tables(256)
    consts = [wave, sign, right_tables()]
    for table in (synth_cos, synth_sin, back_cos, back_sin):
        high, low = two_parts(table)
        consts.append(np.concatenate([high, high, low], axis=1))
    consts = [jnp.asarray(c) for c in consts]

    def whole(array):
        return pl.BlockSpec(array.shape, lambda i: (0,) * array.ndim)

    block = pl.BlockSpec((16, 3, 2, 16, 256), lambda i: (0, 0, 0, 0, i))
    return pl.pallas_call(
        plane_kernel,
        grid=(2,),
        in_specs=[block] + [whole(c) for c in [metric, rate, mask, mass] + consts],
        out_specs=[block, pl.BlockSpec((16, 2, 16, 256), lambda i: (0, 0, 0, i))],
        out_shape=[
            jax.ShapeDtypeStruct((16, 3, 2, 16, 512), F32),
            jax.ShapeDtypeStruct((16, 2, 16, 512), F32),
        ],
        scratch_shapes=[
            pltpu.VMEM((6, 2, 256, 256), BF16),
            pltpu.VMEM((6, 2, 256, 256), BF16),
            pltpu.VMEM((6, 2, 256, 256), F32),
            pltpu.VMEM((3, 2, 256, 256), BF16),
            pltpu.VMEM((3, 2, 256, 256), BF16),
            pltpu.VMEM((3, 8, 256), F32),
            pltpu.VMEM((3, 2, 2, 256, 256), F32),
            pltpu.VMEM((2, 8, 256), F32),
            pltpu.VMEM((6, 128, 128), F32),
        ],
        compiler_params=pltpu.CompilerParams(vmem_limit_bytes=WIDE),
        name="in_planes",
    )(blocks, metric, rate, mask, mass, *consts)


def slopes_of(pair, forward):
    up, down = split(pair)
    both = dot(forward, jnp.concatenate([up, down, up], axis=0))
    return both[:64], both[64:]


def twice(value):
    return jnp.concatenate([value, value], axis=1)


FIELD = (2, 16, 64, 128)
EDGE = (2, 2, 16, 8, 128)


def whole_spec(shape):
    return pl.BlockSpec(shape, lambda i: (0,) * len(shape))


def wave_of(kl):
    return (lax.axis_index("mode") * 16 + kl).astype(F32) * (np.pi / 256)


def turn_back(r_ref, tmp, count):
    half = low_half((count, 128))
    for pair in range(64):
        g, i = divmod(pair, 4)
        cols = slice(128 * i, 128 * i + 128)
        re = r_ref[g, 0, :, cols]
        im = r_ref[g, 1, :, cols]
        place = 2 * count * pair
        tmp[place : place + count, :] = jnp.where(half, re, swap(im))
        tmp[place + count : place + 2 * count, :] = jnp.where(half, swap(re), im)


def right_kernel(r_ref, raw_ref, edge_ref, tmp):
    turn_back(r_ref, tmp, 16)
    for kl in range(16):
        raw_ref[:, kl] = tmp[pl.ds(kl, 128, stride=16), :].T.reshape(2, 64, 128)
        for part in range(2):
            edge_ref[0, part, kl] = raw_ref[part, kl, pl.ds(0, 8, stride=8), :]
            edge_ref[1, part, kl] = raw_ref[part, kl, pl.ds(7, 8, stride=8), :]


def right_side(blocks):
    return pl.pallas_call(
        right_kernel,
        out_shape=[jax.ShapeDtypeStruct(FIELD, F32), jax.ShapeDtypeStruct(EDGE, F32)],
        scratch_shapes=[pltpu.VMEM((2048, 128), F32)],
        compiler_params=pltpu.CompilerParams(vmem_limit_bytes=NARROW),
        cost_estimate=SMALL,
        name="right_side",
    )(blocks)


def post_kernel(r_ref, non_ref, tmp):
    turn_back(r_ref.at[:, 0], tmp, 16)
    for kl in range(16):
        non_ref[0, :, kl] = tmp[pl.ds(kl, 128, stride=16), :].T.reshape(2, 64, 128)


def from_blocks(blocks):
    return pl.pallas_call(
        post_kernel,
        grid=(3,),
        in_specs=[pl.BlockSpec((16, 1, 2, 16, 512), lambda c: (0, c, 0, 0, 0))],
        out_specs=pl.BlockSpec((1, 2, 16, 64, 128), lambda c: (c, 0, 0, 0, 0)),
        out_shape=jax.ShapeDtypeStruct((3, 2, 16, 64, 128), F32),
        scratch_shapes=[pltpu.VMEM((2048, 128), F32)],
        compiler_params=pltpu.CompilerParams(vmem_limit_bytes=NARROW),
        name="from_blocks",
    )(blocks)


def lanes(value, index):
    return jnp.take_along_axis(value, index, axis=1, mode="promise_in_bounds")


def links_of(link_ref):
    device = lax.axis_index("elem")
    links = []
    for side in range(4):
        ident = jnp.broadcast_to(link_ref[side : side + 1, :], (8, 128))
        here = ident >= 0
        if side < 2:
            place = ident - (device - 1) * 128
            origin = place >> 7
            origin = jnp.where((device & 1) == 1, origin, 2 - origin)
            links.append((jnp.where(here, place & 127, 0), jnp.where(here, origin, 3)))
        else:
            links.append((jnp.where(here, ident - device * 128, 0), here))
    return links


def share(out_ref, field_ref, near_edge, far_edge, links, part, kl):
    (west_lane, west_from), (east_lane, east_from), (south_lane, south_here), (north_lane, north_here) = links
    first = field_ref[part, kl, pl.ds(0, 8, stride=8), :]
    last = field_ref[part, kl, pl.ds(7, 8, stride=8), :]

    def pick(side, own, lane, origin):
        value = jnp.where(origin == 1, lanes(own, lane), 0.0)
        value = jnp.where(origin == 0, lanes(near_edge[side, part, kl], lane), value)
        return jnp.where(origin == 2, lanes(far_edge[side, part, kl], lane), value)

    out_ref[part, kl] = field_ref[part, kl]
    out_ref[part, kl, pl.ds(0, 8, stride=8), :] = first + pick(1, last, west_lane, west_from)
    out_ref[part, kl, pl.ds(7, 8, stride=8), :] = last + pick(0, first, east_lane, east_from)
    bottom = out_ref[part, kl, 0:8, :]
    top = out_ref[part, kl, 56:64, :]
    out_ref[part, kl, 0:8, :] = bottom + jnp.where(south_here, lanes(top, south_lane), 0.0)
    out_ref[part, kl, 56:64, :] = top + jnp.where(north_here, lanes(bottom, north_lane), 0.0)


def set_stiff(stiff, metric_ref, mass_ref):
    mass = mass_ref[...]
    rx, ry, sx, sy = metric_ref[0], metric_ref[1], metric_ref[2], metric_ref[3]
    stiff[0] = mass * (rx * rx + ry * ry)
    stiff[1] = mass * (rx * sx + ry * sy)
    stiff[2] = mass * (sx * sx + sy * sy)


def set_inverse(inverse, link_ref):
    node = lax.broadcasted_iota(jnp.int32, (64, 128), 0)
    here = [link_ref[side : side + 1, :] >= 0 for side in range(4)]
    places = [(node & 7) == 0, (node & 7) == 7, node < 8, node >= 56]
    value = jnp.ones((64, 128), F32)
    for place, there in zip(places, here):
        value = jnp.where(place & there, 0.5 * value, value)
    inverse[...] = value


def stiffness(pair, shift, stiff, mass_ref, fwd_ref, adj_ref, adl_ref):
    along_r, along_s = slopes_of(pair, fwd_ref[...])
    cross = twice(stiff[1])
    back = jnp.concatenate(
        [
            twice(stiff[0]) * along_r + cross * along_s,
            cross * along_r + twice(stiff[2]) * along_s,
        ],
        axis=0,
    )
    up, down = split(back)
    folded = dot(adj_ref[...], jnp.concatenate([up, down], axis=0)) + dot(adl_ref[...], up)
    return folded + shift * twice(mass_ref[...]) * pair


def image_kernel(
    raw_ref, near_edge, far_edge, link_ref, metric_ref, mass_ref, fwd_ref, adj_ref, adl_ref,
    field_ref, image_ref, edge_ref, stiff,
):
    links = links_of(link_ref)
    set_stiff(stiff, metric_ref, mass_ref)
    for kl in range(16):
        for part in range(2):
            share(field_ref, raw_ref, near_edge, far_edge, links, part, kl)
    for kl in range(16):
        pair = jnp.concatenate([field_ref[0, kl], field_ref[1, kl]], axis=1)
        wave = wave_of(kl)
        image = stiffness(pair, wave * wave + 1.0, stiff, mass_ref, fwd_ref, adj_ref, adl_ref)
        for part in range(2):
            image_ref[part, kl] = image[:, 128 * part : 128 * part + 128]
            edge_ref[0, part, kl] = image_ref[part, kl, pl.ds(0, 8, stride=8), :]
            edge_ref[1, part, kl] = image_ref[part, kl, pl.ds(7, 8, stride=8), :]


def image_of(raw, near, far, links, metric, mass, left):
    return pl.pallas_call(
        image_kernel,
        in_specs=[pl.BlockSpec(memory_space=pltpu.VMEM)] * 9,
        out_shape=[
            jax.ShapeDtypeStruct(FIELD, F32),
            jax.ShapeDtypeStruct(FIELD, F32),
            jax.ShapeDtypeStruct(EDGE, F32),
        ],
        scratch_shapes=[pltpu.VMEM((3, 64, 128), F32)],
        compiler_params=pltpu.CompilerParams(vmem_limit_bytes=NARROW),
        cost_estimate=SMALL,
        name="image",
    )(raw, near, far, links, metric, mass, *left)


def folded_rows(value):
    return jnp.sum(value[0] + value[1], axis=0, keepdims=True)


def moments_kernel(
    image_ref, near_edge, far_edge, field_ref, link_ref, metric_ref, mass_ref, fwd_ref, adj_ref,
    adl_ref, shared_ref, sum_ref, stiff, inverse, second, rows, local,
):
    links = links_of(link_ref)
    set_stiff(stiff, metric_ref, mass_ref)
    set_inverse(inverse, link_ref)
    for kl in range(16):
        for part in range(2):
            share(shared_ref, image_ref, near_edge, far_edge, links, part, kl)
    for kl in range(16):
        pair = jnp.concatenate([shared_ref[0, kl], shared_ref[1, kl]], axis=1)
        wave = wave_of(kl)
        image = stiffness(pair, wave * wave + 1.0, stiff, mass_ref, fwd_ref, adj_ref, adl_ref)
        for part in range(2):
            second[part, kl] = image[:, 128 * part : 128 * part + 128]
        weighed = shared_ref[:, kl] * inverse[...]
        rows[0, kl : kl + 1, :] = folded_rows(weighed * field_ref[:, kl])
        rows[1, kl : kl + 1, :] = folded_rows(weighed * shared_ref[:, kl])
    cross = jnp.sum(rows[0], axis=1, keepdims=True)
    square = jnp.sum(rows[1], axis=1, keepdims=True)
    guess = jnp.where(square > 0.0, cross / jnp.where(square > 0.0, square, 1.0), 0.0)
    local[...] = jnp.broadcast_to(guess, (16, 128))
    for kl in range(16):
        step = local[kl : kl + 1, :]
        one = shared_ref[:, kl]
        two = second[:, kl]
        left = field_ref[:, kl] - step * one
        image = image_ref[:, kl] - step * two
        weighed = left * inverse[...]
        rows[0, kl : kl + 1, :] = folded_rows(left * weighed)
        rows[2, kl : kl + 1, :] = folded_rows(one * weighed)
        rows[3, kl : kl + 1, :] = folded_rows(left * image)
        rows[4, kl : kl + 1, :] = folded_rows(left * two + one * image)
        rows[5, kl : kl + 1, :] = folded_rows(one * two)
    place = lax.broadcasted_iota(jnp.int32, (16, 128), 1)
    packed = local[...]
    for q, row in enumerate((0, 2, 1, 3, 4, 5)):
        packed = jnp.where(place == q + 1, jnp.sum(rows[row], axis=1, keepdims=True), packed)
    sum_ref[0] = packed


def moments_of(image, near, far, field, links, metric, mass, left):
    return pl.pallas_call(
        moments_kernel,
        in_specs=[pl.BlockSpec(memory_space=pltpu.VMEM)] * 10,
        out_shape=[jax.ShapeDtypeStruct(FIELD, F32), jax.ShapeDtypeStruct((1, 16, 128), F32)],
        scratch_shapes=[
            pltpu.VMEM((3, 64, 128), F32),
            pltpu.VMEM((64, 128), F32),
            pltpu.VMEM(FIELD, F32),
            pltpu.VMEM((6, 16, 128), F32),
            pltpu.VMEM((16, 128), F32),
        ],
        compiler_params=pltpu.CompilerParams(vmem_limit_bytes=NARROW),
        cost_estimate=SMALL,
        name="moments",
    )(image, near, far, field, links, metric, mass, *left)


def final_kernel(field_ref, shared_ref, sum_ref, out_ref, scales):
    packed = sum_ref[...]
    place = lax.broadcasted_iota(jnp.int32, packed.shape, 2)
    guess, left2, cross, square, energy, mixed, second = [
        jnp.broadcast_to(
            jnp.sum(jnp.where(place == q, packed, 0.0), axis=2, keepdims=True), packed.shape
        )
        for q in range(7)
    ]
    norm0 = jnp.sum(left2 + guess * (2.0 * cross + guess * square), axis=0)
    energy0 = jnp.sum(cross + guess * square, axis=0)
    alpha0 = norm0 / energy0
    off = guess - alpha0[None]
    norm1 = jnp.sum(left2 + off * (2.0 * cross + off * square), axis=0)
    energy1 = jnp.sum(energy + off * (mixed + off * second), axis=0)
    beta = norm1 / norm0
    alpha1 = norm1 / (energy1 - beta * norm1 / alpha0)
    scales[0] = alpha0 + alpha1 * (1.0 + beta)
    scales[1] = -alpha1 * alpha0
    for kl in range(16):
        one = scales[0, kl : kl + 1, :]
        two = scales[1, kl : kl + 1, :]
        out_ref[:, kl] = one * field_ref[:, kl] + two * shared_ref[:, kl]


def final(field, shared, sums):
    return pl.pallas_call(
        final_kernel,
        out_shape=jax.ShapeDtypeStruct(FIELD, F32),
        scratch_shapes=[pltpu.VMEM((2, 16, 128), F32)],
        compiler_params=pltpu.CompilerParams(vmem_limit_bytes=NARROW),
        cost_estimate=SMALL,
        name="pressure",
    )(field, shared, sums)


def swap_edges(edges):
    count = lax.axis_size("elem")
    far = [pair for i in range(1, count - 1, 2) for pair in ((i, i + 1), (i + 1, i))]
    far = lax.ppermute(edges, "elem", far)
    near = lax.ppermute(edges, "elem", [(i, i ^ 1) for i in range(count)])
    return near, far


def gather_sums(sums):
    count = lax.axis_size("elem")
    for step in (1, 2, 4):
        other = lax.ppermute(sums, "elem", [(i, i ^ step) for i in range(count)])
        sums = jnp.concatenate([sums, other], axis=0)
    return sums


def over(array, axis):
    return lax.all_to_all(array, axis, split_axis=0, concat_axis=0, tiled=True)


def per_device(velocity, metric, mass, sponge_rate, sponge_mask, neighbours):
    left = [jnp.asarray(t) for t in left_tables()]

    blocks = over(to_blocks(velocity), "mode")
    blocks, raw = in_planes(blocks, metric, sponge_rate, sponge_mask.reshape(1, 128), mass)
    raw = over(raw, "mode")
    blocks, raw = lax.optimization_barrier((blocks, raw))
    blocks = over(blocks, "mode")
    raw, edges = right_side(raw)
    near, far = swap_edges(edges)
    field, image, edges = image_of(raw, near, far, neighbours, metric, mass, left)
    near, far = swap_edges(edges)
    shared, sums = moments_of(image, near, far, field, neighbours, metric, mass, left)
    return from_blocks(blocks), final(field, shared, gather_sums(sums))


def solution(mesh):
    return jax.shard_map(
        per_device,
        mesh=mesh,
        in_specs=(
            P(None, None, "mode", None, "elem"),
            P(None, None, "elem"),
            P(None, "elem"),
            P(None, "elem"),
            P("elem"),
            P(None, "elem"),
        ),
        out_specs=(P(None, None, "mode", None, "elem"), P(None, "mode", None, "elem")),
        check_vma=False,
    )
```

```python
import jax
import jax.numpy as jnp
import ml_dtypes
import numpy as np
from jax import lax
from jax.experimental import pallas as pl
from jax.experimental.pallas import tpu as pltpu
from jax.sharding import PartitionSpec as P

F32 = jnp.float32
BF16 = jnp.bfloat16
MIB = 1024 * 1024
WIDE = 48 * MIB
BLOCKS = (16, 3, 128, 128)
NARROW = 16 * MIB
SMALL = pl.CostEstimate(flops=1000, bytes_accessed=1000, transcendentals=0)


def cheb_matrix():
    count = 8
    places = np.arange(count)
    points = np.cos(np.pi * places / (count - 1))
    weights = np.where((places == 0) | (places == count - 1), 2.0, 1.0)
    signs = weights * (-1.0) ** places
    differ = points[:, None] - points[None, :] + np.eye(count)
    table = np.outer(signs, 1.0 / signs) / differ
    table = table - np.eye(count) * np.sum(table, axis=1)[:, None]
    return table.astype(np.float32).astype(np.float64)


def two_parts(table):
    high = table.astype(np.float32).astype(ml_dtypes.bfloat16)
    low = (table - high.astype(np.float64)).astype(np.float32).astype(ml_dtypes.bfloat16)
    return high, low


def mode_order(modes):
    row = np.arange(modes)
    return 16 * ((row % (modes // 2)) // 8) + 2 * (row % 8) + row // (modes // 2)


def tables(modes):
    planes = 2 * modes
    half = modes // 2
    order = mode_order(modes)
    even, odd = order[:half], order[half:]
    spots = np.arange(half)

    def angles(places, ks):
        return ((places[:, None] * ks[None, :]) % planes) * (2.0 * np.pi / planes)

    quarter = np.array([half])
    weight_even = np.where(even == 0, 1.0, 2.0)
    extra = np.zeros((16, half))
    extra[:1] = weight_even * np.cos(angles(quarter, even))
    cos_even = np.concatenate([weight_even * np.cos(angles(spots, even)), extra], axis=0)
    cos_odd = 2.0 * np.cos(angles(spots, odd))
    sin_even = weight_even * np.sin(angles(spots, even))
    sin_odd = 2.0 * np.sin(angles(spots, odd))
    sin_odd[:1] = 2.0 * np.sin(angles(quarter, odd))
    back_cos_even = np.cos(angles(spots, even)).T / planes
    back_cos_odd = np.cos(angles(spots, odd)).T / planes
    back_sin_even = -np.sin(angles(spots, even)).T / planes
    back_sin_odd = -np.sin(angles(spots, odd)).T / planes
    back_sin_odd[:, :1] = -np.sin(angles(quarter, odd)).T / planes
    wave = np.broadcast_to((order * np.pi / modes)[:, None], (modes, 128)).astype(np.float32)
    sign = np.round(np.cos(angles(quarter, even)).T) / planes
    sign = np.broadcast_to(sign, (half, 128)).astype(np.float32)
    there = [cos_even, cos_odd, sin_even, sin_odd]
    back = [back_cos_even, back_cos_odd, back_sin_even, back_sin_odd]
    return there, back, wave, sign


def right_tables():
    table = cheb_matrix()
    two = np.eye(2)
    eight = np.eye(8)
    along_r = np.kron(two, np.kron(eight, table.T))
    along_s = np.kron(two, np.kron(table.T, eight))
    high, low = two_parts(np.concatenate([along_r, along_s], axis=1))
    return np.concatenate([high, high, low], axis=0)


def left_tables():
    table = cheb_matrix()
    eight = np.eye(8)
    along_r = np.kron(eight, table)
    along_s = np.kron(table, eight)
    high, low = two_parts(np.concatenate([along_r, along_s], axis=0))
    forward = np.concatenate([high, high, low], axis=1)
    high, low = two_parts(np.concatenate([along_r.T, along_s.T], axis=1))
    return forward, np.concatenate([high, high], axis=1), low


def split(value):
    high = value.astype(BF16)
    low = (value - high.astype(F32)).astype(BF16)
    return high, low


def dot(first, second):
    return jnp.dot(first, second, preferred_element_type=F32)


def low_half(shape):
    return lax.broadcasted_iota(jnp.int32, shape, len(shape) - 1) < 64


def swap(value):
    return pltpu.roll(value, 64, 1)


def spot(kl):
    return 8 * (kl % 2) + kl // 2


def pre_kernel(v_all, y_ref, v_ref, sems):
    def fetch(c, h):
        part = pl.ds(8 * h, 8)
        return pltpu.make_async_copy(v_all.at[c, :, part], v_ref.at[c, :, part], sems.at[c, h])

    pieces = [(c, h) for c in range(3) for h in range(2)]
    for piece in pieces:
        fetch(*piece).start()
    for c, h in pieces:
        fetch(c, h).wait()
        for kl in range(8 * h, 8 * h + 8):
            turned = v_ref[c, :, kl].reshape(128, 128).T
            for g in range(16):
                y_ref[g, c, pl.ds(spot(kl), 8, stride=16), :] = turned[8 * g : 8 * g + 8, :]


def to_blocks(velocity):
    return pl.pallas_call(
        pre_kernel,
        in_specs=[pl.BlockSpec(memory_space=pl.ANY)],
        out_specs=pl.BlockSpec(memory_space=pltpu.VMEM),
        out_shape=jax.ShapeDtypeStruct(BLOCKS, F32),
        scratch_shapes=[pltpu.VMEM((3, 2, 16, 64, 128), F32), pltpu.SemaphoreType.DMA((3, 2))],
        compiler_params=pltpu.CompilerParams(vmem_limit_bytes=48 * MIB),
        name="to_blocks",
    )(velocity)


ROWS = 32


def node_rows(rows, tmp, metric_ref, rate_ref, mask_ref, mass_ref):
    place = pl.multiple_of(lax.axis_index("mode") * 8, 8)
    damping = mask_ref[...].astype(F32) * rate_ref[...]
    blank = jnp.zeros((64, 128), F32)
    values = [metric_ref[0], metric_ref[1], metric_ref[2], metric_ref[3], damping, mass_ref[...]]
    for q, value in enumerate(values):
        tmp[q] = jnp.concatenate([value, blank], axis=0).T
    for q in range(6):
        mine = tmp[q, pl.ds(place, 8), :]
        other = swap(mine)
        for i in range(4):
            row = mine[2 * i : 2 * i + 1, :] + other[2 * i + 1 : 2 * i + 2, :]
            rows[i // 2, q : q + 1, 128 * (i % 2) : 128 * (i % 2) + 128] = row


def stacked(high, low):
    return jnp.concatenate([high, low, high], axis=0)


def plane_kernel(
    z_all, metric_ref, rate_ref, mask_ref, mass_ref, wave_ref, sign_ref, slope_ref, ce_ref, co_ref,
    se_ref, so_ref, bce_ref, bco_ref, bse_ref, bso_ref, out_all, raw_ref, z_ref, out_ref, high, low, planes, eh, el,
    tail, grads, flat, rows_all, turned, z_sem,
    out_sem,
):
    def fetch(i, c):
        part = pl.ds(pl.multiple_of(64 * i, 64), 64)
        return pltpu.make_async_copy(z_all.at[:, c, part, :], z_ref.at[:, c, part, :], z_sem.at[i, c])

    def store(i):
        part = pl.ds(pl.multiple_of(64 * i, 64), 64)
        return pltpu.make_async_copy(out_ref.at[i], out_all.at[:, :, part, :], out_sem.at[i])

    for i in range(2):
        for c in range(3):
            fetch(i, c).start()
    node_rows(rows_all, turned, metric_ref, rate_ref, mask_ref, mass_ref)

    def one_half(i, carry):
        half_kernel(
            i, fetch, store, z_ref, wave_ref, sign_ref, slope_ref, ce_ref, co_ref, se_ref, so_ref, bce_ref, bco_ref,
            bse_ref, bso_ref, out_ref.at[i], raw_ref, high, low, planes, eh, el, tail, grads, flat, rows_all,
        )
        return carry

    lax.fori_loop(0, 2, one_half, 0)
    for i in range(2):
        store(i).wait()


def half_kernel(
    i, fetch, store, z_ref, wave_ref, sign_ref, slope_ref, ce_ref, co_ref, se_ref, so_ref, bce_ref, bco_ref,
    bse_ref, bso_ref, out_ref, raw_ref, high, low, planes, eh, el, tail, grads, flat, rows_all,
):
    base = pl.multiple_of(64 * i, 64)
    node = rows_all[i]
    rx = node[0:1, :]
    ry = node[1:2, :]
    sx = node[2:3, :]
    sy = node[3:4, :]
    damping = node[4:5, :]
    mass = node[5:6, :]
    half = low_half((256, 128))

    def trade(first, second):
        return jnp.where(half, first, swap(second)), jnp.where(half, swap(first), second)

    def cells(c, place):
        return jnp.concatenate(
            [z_ref[:, c, pl.ds(base + place + 8 * p, 8), :].reshape(128, 128) for p in range(2)], axis=0
        )

    def slopes(c, part, q, up, down):
        cols = slice(128 * q, 128 * q + 128)
        both = dot(jnp.concatenate([up, down, up], axis=1), slope_ref[...])
        grads[c, part, 0, :, cols] = both[:, :128]
        grads[c, part, 1, :, cols] = both[:, 128:]

    for c in range(3):
        fetch(i, c).wait()
        for q in range(2):
            cols = slice(128 * q, 128 * q + 128)
            for part, value in enumerate(trade(cells(c, 32 * q), cells(c, 32 * q + 16))):
                if c < 2:
                    flat[c, part, :, cols] = value
                up, down = split(value)
                high[c, part, :, cols] = up
                low[c, part, :, cols] = down
    for c in range(3):
        for part in range(2):
            for q in range(2):
                cols = slice(128 * q, 128 * q + 128)
                slopes(c, part, q, high[c, part, :, cols], low[c, part, :, cols])

    for step in range(256 // ROWS):
        rows = slice(step * ROWS, step * ROWS + ROWS)
        wave = twice(wave_ref[rows, :])
        for part in range(2):
            u_r, u_s = grads[0, part, 0, rows, :], grads[0, part, 1, rows, :]
            v_r, v_s = grads[1, part, 0, rows, :], grads[1, part, 1, rows, :]
            w_r, w_s = grads[2, part, 0, rows, :], grads[2, part, 1, rows, :]
            u_t = flat[0, 1 - part, rows, :]
            v_t = flat[1, 1 - part, rows, :]
            turn = -wave if part == 0 else wave
            swirl = (
                ry * w_r + sy * w_s - turn * v_t,
                turn * u_t - (rx * w_r + sx * w_s),
                rx * v_r + sx * v_s - (ry * u_r + sy * u_s),
            )
            for c in range(3):
                up, down = split(swirl[c])
                high[3 + c, part, rows, :] = up
                low[3 + c, part, rows, :] = down

    for c in range(6):
        ce = dot(ce_ref[...], stacked(high[c, 0, :128], low[c, 0, :128]))
        co = dot(co_ref[...], stacked(high[c, 0, 128:], low[c, 0, 128:]))
        se = dot(se_ref[...], stacked(high[c, 1, :128], low[c, 1, :128]))
        so = dot(so_ref[...], stacked(high[c, 1, 128:], low[c, 1, 128:]))
        top, bottom = ce[:128] + co, ce[:128] - co
        add, sub = se + so, se - so
        planes[c, 0] = top - add
        planes[c, 1] = top + add
        planes[c, 2] = bottom + sub
        planes[c, 3] = bottom - sub
        planes[c, 0, 0:1, :] = ce[0:1] + co[0:1]
        planes[c, 1, 0:1, :] = ce[128:129] - so[0:1]
        planes[c, 2, 0:1, :] = ce[0:1] - co[0:1]
        planes[c, 3, 0:1, :] = ce[128:129] + so[0:1]

    def force(u, w):
        return (
            u[1] * w[2] - u[2] * w[1] - damping * (u[0] - 1.0),
            u[2] * w[0] - u[0] * w[2] - damping * u[1],
            u[0] * w[1] - u[1] * w[0] - damping * u[2],
        )

    first_row = lax.broadcasted_iota(jnp.int32, (ROWS, 256), 0) == 0
    for step in range(128 // ROWS):
        rows = slice(step * ROWS, step * ROWS + ROWS)
        quads = []
        for quad in range(4):
            here = [planes[c, quad, rows, :] for c in range(6)]
            quads.append(force(here[:3], here[3:]))
        for c in range(3):
            one, two, three, four = [quad[c] for quad in quads]
            plus, minus = one + two, one - two
            more, less = three + four, three - four
            sums = [plus + more, plus - more, minus - less, minus + less]
            if step == 0:
                sums[0] = jnp.where(first_row, one + three, sums[0])
                sums[1] = jnp.where(first_row, one - three, sums[1])
                sums[3] = jnp.where(first_row, two - four, sums[3])
                tail[c, 0:8, :] = (two + four)[0:8, :]
            for quad in range(4):
                up, down = split(sums[quad])
                eh[c, quad, rows, :] = up
                el[c, quad, rows, :] = down

    backs = (bce_ref, bco_ref, bse_ref, bso_ref)
    for c in range(3):
        for quad in range(4):
            value = dot(backs[quad][...], stacked(eh[c, quad], el[c, quad]))
            if quad == 0:
                value = value + twice(sign_ref[...]) * tail[c, 0:1, :]
            flat[c, quad // 2, 128 * (quad % 2) : 128 * (quad % 2) + 128, :] = value
    def put(ref, place, value):
        for p in range(2):
            ref[:, pl.ds(place + 8 * p, 8), :] = value[128 * p : 128 * p + 128].reshape(16, 8, 128)

    for c in range(3):
        for q in range(2):
            cols = slice(128 * q, 128 * q + 128)
            first, second = trade(flat[c, 0, :, cols], flat[c, 1, :, cols])
            put(out_ref.at[:, c], 32 * q, first)
            put(out_ref.at[:, c], 32 * q + 16, second)
    store(i).start()
    for c in range(2):
        for part in range(2):
            for q in range(2):
                slopes(c, part, q, *split(flat[c, part, :, 128 * q : 128 * q + 128]))

    x_r, x_s, y_r, y_s = -mass * rx, -mass * sx, -mass * ry, -mass * sy
    for q in range(2):
        cols = slice(128 * q, 128 * q + 128)
        values = []
        for part in range(2):
            turn = wave_ref[...] if part == 0 else -wave_ref[...]
            values.append(
                x_r[:, cols] * grads[0, part, 0, :, cols]
                + x_s[:, cols] * grads[0, part, 1, :, cols]
                + y_r[:, cols] * grads[1, part, 0, :, cols]
                + y_s[:, cols] * grads[1, part, 1, :, cols]
                + mass[:, cols] * (turn * flat[2, 1 - part, :, cols])
            )
        first, second = trade(*values)
        put(raw_ref, base + 32 * q, first)
        put(raw_ref, base + 32 * q + 16, second)


def in_planes(blocks, metric, rate, mask, mass):
    there, back, wave, sign = tables(256)
    consts = [wave, sign, right_tables()]
    for table in there + back:
        high, low = two_parts(table)
        consts.append(np.concatenate([high, high, low], axis=1))
    consts = [jnp.asarray(c) for c in consts]

    in_vmem = pl.BlockSpec(memory_space=pltpu.VMEM)
    return pl.pallas_call(
        plane_kernel,
        in_specs=[pl.BlockSpec(memory_space=pl.ANY)] + [in_vmem] * (4 + len(consts)),
        out_specs=[pl.BlockSpec(memory_space=pl.ANY), in_vmem],
        out_shape=[
            jax.ShapeDtypeStruct(BLOCKS, F32),
            jax.ShapeDtypeStruct((16, 128, 128), F32),
        ],
        scratch_shapes=[
            pltpu.VMEM(BLOCKS, F32),
            pltpu.VMEM((2, 16, 3, 64, 128), F32),
            pltpu.VMEM((6, 2, 256, 256), BF16),
            pltpu.VMEM((6, 2, 256, 256), BF16),
            pltpu.VMEM((6, 4, 128, 256), F32),
            pltpu.VMEM((3, 4, 128, 256), BF16),
            pltpu.VMEM((3, 4, 128, 256), BF16),
            pltpu.VMEM((3, 8, 256), F32),
            pltpu.VMEM((3, 2, 2, 256, 256), F32),
            pltpu.VMEM((3, 2, 256, 256), F32),
            pltpu.VMEM((2, 8, 256), F32),
            pltpu.VMEM((6, 128, 128), F32),
            pltpu.SemaphoreType.DMA((2, 3)),
            pltpu.SemaphoreType.DMA((2,)),
        ],
        compiler_params=pltpu.CompilerParams(vmem_limit_bytes=50 * MIB),
        name="in_planes",
    )(blocks, metric, rate, mask, mass, *consts)


def slopes_of(pair, forward):
    up, down = split(pair)
    both = dot(forward, jnp.concatenate([up, down, up], axis=0))
    return both[:64], both[64:]


def twice(value):
    return jnp.concatenate([value, value], axis=1)


FIELD = (2, 16, 64, 128)
EDGE = (2, 2, 16, 8, 128)


def whole_spec(shape):
    return pl.BlockSpec(shape, lambda i: (0,) * len(shape))


def wave_of(kl):
    return (lax.axis_index("mode") * 16 + kl).astype(F32) * (np.pi / 256)


def right_kernel(r_ref, raw_ref, edge_ref):
    for kl in range(16):
        block = jnp.concatenate([r_ref[g, pl.ds(spot(kl), 8, stride=16), :] for g in range(16)], axis=0)
        raw_ref[:, kl] = block.T.reshape(2, 64, 128)
        for part in range(2):
            edge_ref[0, part, kl] = raw_ref[part, kl, pl.ds(0, 8, stride=8), :]
            edge_ref[1, part, kl] = raw_ref[part, kl, pl.ds(7, 8, stride=8), :]


def right_side(blocks):
    return pl.pallas_call(
        right_kernel,
        out_shape=[jax.ShapeDtypeStruct(FIELD, F32), jax.ShapeDtypeStruct(EDGE, F32)],
        compiler_params=pltpu.CompilerParams(vmem_limit_bytes=NARROW),
        cost_estimate=SMALL,
        name="right_side",
    )(blocks)


def post_kernel(r_ref, non_all, non_ref, sems):
    def store(c, h):
        part = pl.ds(8 * h, 8)
        return pltpu.make_async_copy(non_ref.at[c, :, part], non_all.at[c, :, part], sems.at[c, h])

    pieces = [(c, h) for c in range(3) for h in range(2)]
    for c, h in pieces:
        for kl in range(8 * h, 8 * h + 8):
            block = jnp.concatenate([r_ref[g, c, pl.ds(spot(kl), 8, stride=16), :] for g in range(16)], axis=0)
            non_ref[c, :, kl] = block.T.reshape(2, 64, 128)
        store(c, h).start()
    for piece in pieces:
        store(*piece).wait()


def from_blocks(blocks):
    return pl.pallas_call(
        post_kernel,
        in_specs=[pl.BlockSpec(memory_space=pltpu.VMEM)],
        out_specs=pl.BlockSpec(memory_space=pl.ANY),
        out_shape=jax.ShapeDtypeStruct((3, 2, 16, 64, 128), F32),
        scratch_shapes=[pltpu.VMEM((3, 2, 16, 64, 128), F32), pltpu.SemaphoreType.DMA((3, 2))],
        compiler_params=pltpu.CompilerParams(vmem_limit_bytes=NARROW),
        name="from_blocks",
    )(blocks)


def lanes(value, index):
    return jnp.take_along_axis(value, index, axis=1, mode="promise_in_bounds")


def links_of(link_ref):
    device = lax.axis_index("elem")
    links = []
    for side in range(4):
        ident = jnp.broadcast_to(link_ref[side : side + 1, :], (8, 128))
        here = ident >= 0
        if side < 2:
            place = ident - (device - 1) * 128
            origin = place >> 7
            origin = jnp.where((device & 1) == 1, origin, 2 - origin)
            links.append((jnp.where(here, place & 127, 0), jnp.where(here, origin, 3)))
        else:
            links.append((jnp.where(here, ident - device * 128, 0), here))
    return links


def share(out_ref, field_ref, near_edge, far_edge, links, part, kl):
    (west_lane, west_from), (east_lane, east_from), (south_lane, south_here), (north_lane, north_here) = links
    first = field_ref[part, kl, pl.ds(0, 8, stride=8), :]
    last = field_ref[part, kl, pl.ds(7, 8, stride=8), :]

    def pick(side, own, lane, origin):
        value = jnp.where(origin == 1, lanes(own, lane), 0.0)
        value = jnp.where(origin == 0, lanes(near_edge[side, part, kl], lane), value)
        return jnp.where(origin == 2, lanes(far_edge[side, part, kl], lane), value)

    out_ref[part, kl] = field_ref[part, kl]
    out_ref[part, kl, pl.ds(0, 8, stride=8), :] = first + pick(1, last, west_lane, west_from)
    out_ref[part, kl, pl.ds(7, 8, stride=8), :] = last + pick(0, first, east_lane, east_from)
    bottom = out_ref[part, kl, 0:8, :]
    top = out_ref[part, kl, 56:64, :]
    out_ref[part, kl, 0:8, :] = bottom + jnp.where(south_here, lanes(top, south_lane), 0.0)
    out_ref[part, kl, 56:64, :] = top + jnp.where(north_here, lanes(bottom, north_lane), 0.0)


def set_stiff(stiff, metric_ref, mass_ref):
    mass = mass_ref[...]
    rx, ry, sx, sy = metric_ref[0], metric_ref[1], metric_ref[2], metric_ref[3]
    stiff[0] = mass * (rx * rx + ry * ry)
    stiff[1] = mass * (rx * sx + ry * sy)
    stiff[2] = mass * (sx * sx + sy * sy)


def set_inverse(inverse, link_ref):
    node = lax.broadcasted_iota(jnp.int32, (64, 128), 0)
    here = [link_ref[side : side + 1, :] >= 0 for side in range(4)]
    places = [(node & 7) == 0, (node & 7) == 7, node < 8, node >= 56]
    value = jnp.ones((64, 128), F32)
    for place, there in zip(places, here):
        value = jnp.where(place & there, 0.5 * value, value)
    inverse[...] = value


def stiffness(pair, shift, stiff, mass_ref, fwd_ref, adj_ref, adl_ref):
    along_r, along_s = slopes_of(pair, fwd_ref[...])
    cross = twice(stiff[1])
    back = jnp.concatenate(
        [
            twice(stiff[0]) * along_r + cross * along_s,
            cross * along_r + twice(stiff[2]) * along_s,
        ],
        axis=0,
    )
    up, down = split(back)
    folded = dot(adj_ref[...], jnp.concatenate([up, down], axis=0)) + dot(adl_ref[...], up)
    return folded + shift * twice(mass_ref[...]) * pair


def image_kernel(
    raw_ref, near_edge, far_edge, link_ref, metric_ref, mass_ref, fwd_ref, adj_ref, adl_ref,
    field_ref, image_ref, edge_ref, stiff,
):
    links = links_of(link_ref)
    set_stiff(stiff, metric_ref, mass_ref)
    for kl in range(16):
        for part in range(2):
            share(field_ref, raw_ref, near_edge, far_edge, links, part, kl)
    for kl in range(16):
        pair = jnp.concatenate([field_ref[0, kl], field_ref[1, kl]], axis=1)
        wave = wave_of(kl)
        image = stiffness(pair, wave * wave + 1.0, stiff, mass_ref, fwd_ref, adj_ref, adl_ref)
        for part in range(2):
            image_ref[part, kl] = image[:, 128 * part : 128 * part + 128]
            edge_ref[0, part, kl] = image_ref[part, kl, pl.ds(0, 8, stride=8), :]
            edge_ref[1, part, kl] = image_ref[part, kl, pl.ds(7, 8, stride=8), :]


def image_of(raw, near, far, links, metric, mass, left):
    return pl.pallas_call(
        image_kernel,
        in_specs=[pl.BlockSpec(memory_space=pltpu.VMEM)] * 9,
        out_shape=[
            jax.ShapeDtypeStruct(FIELD, F32),
            jax.ShapeDtypeStruct(FIELD, F32),
            jax.ShapeDtypeStruct(EDGE, F32),
        ],
        scratch_shapes=[pltpu.VMEM((3, 64, 128), F32)],
        compiler_params=pltpu.CompilerParams(vmem_limit_bytes=NARROW),
        cost_estimate=SMALL,
        name="image",
    )(raw, near, far, links, metric, mass, *left)


def folded_rows(value):
    return jnp.sum(value[0] + value[1], axis=0, keepdims=True)


def moments_kernel(
    image_ref, near_edge, far_edge, field_ref, link_ref, metric_ref, mass_ref, fwd_ref, adj_ref,
    adl_ref, shared_ref, sum_ref, stiff, inverse, second, rows, local,
):
    links = links_of(link_ref)
    set_stiff(stiff, metric_ref, mass_ref)
    set_inverse(inverse, link_ref)
    for kl in range(16):
        for part in range(2):
            share(shared_ref, image_ref, near_edge, far_edge, links, part, kl)
    for kl in range(16):
        pair = jnp.concatenate([shared_ref[0, kl], shared_ref[1, kl]], axis=1)
        wave = wave_of(kl)
        image = stiffness(pair, wave * wave + 1.0, stiff, mass_ref, fwd_ref, adj_ref, adl_ref)
        for part in range(2):
            second[part, kl] = image[:, 128 * part : 128 * part + 128]
        weighed = shared_ref[:, kl] * inverse[...]
        rows[0, kl : kl + 1, :] = folded_rows(weighed * field_ref[:, kl])
        rows[1, kl : kl + 1, :] = folded_rows(weighed * shared_ref[:, kl])
    cross = jnp.sum(rows[0], axis=1, keepdims=True)
    square = jnp.sum(rows[1], axis=1, keepdims=True)
    guess = jnp.where(square > 0.0, cross / jnp.where(square > 0.0, square, 1.0), 0.0)
    local[...] = jnp.broadcast_to(guess, (16, 128))
    for kl in range(16):
        step = local[kl : kl + 1, :]
        one = shared_ref[:, kl]
        two = second[:, kl]
        left = field_ref[:, kl] - step * one
        image = image_ref[:, kl] - step * two
        weighed = left * inverse[...]
        rows[0, kl : kl + 1, :] = folded_rows(left * weighed)
        rows[2, kl : kl + 1, :] = folded_rows(one * weighed)
        rows[3, kl : kl + 1, :] = folded_rows(left * image)
        rows[4, kl : kl + 1, :] = folded_rows(left * two + one * image)
        rows[5, kl : kl + 1, :] = folded_rows(one * two)
    place = lax.broadcasted_iota(jnp.int32, (16, 128), 1)
    packed = local[...]
    for q, row in enumerate((0, 2, 1, 3, 4, 5)):
        packed = jnp.where(place == q + 1, jnp.sum(rows[row], axis=1, keepdims=True), packed)
    sum_ref[0] = packed


def moments_of(image, near, far, field, links, metric, mass, left):
    return pl.pallas_call(
        moments_kernel,
        in_specs=[pl.BlockSpec(memory_space=pltpu.VMEM)] * 10,
        out_shape=[jax.ShapeDtypeStruct(FIELD, F32), jax.ShapeDtypeStruct((1, 16, 128), F32)],
        scratch_shapes=[
            pltpu.VMEM((3, 64, 128), F32),
            pltpu.VMEM((64, 128), F32),
            pltpu.VMEM(FIELD, F32),
            pltpu.VMEM((6, 16, 128), F32),
            pltpu.VMEM((16, 128), F32),
        ],
        compiler_params=pltpu.CompilerParams(vmem_limit_bytes=NARROW),
        cost_estimate=SMALL,
        name="moments",
    )(image, near, far, field, links, metric, mass, *left)


def final_kernel(field_ref, shared_ref, sum_ref, out_ref, scales):
    packed = sum_ref[...]
    place = lax.broadcasted_iota(jnp.int32, packed.shape, 2)
    guess, left2, cross, square, energy, mixed, second = [
        jnp.broadcast_to(
            jnp.sum(jnp.where(place == q, packed, 0.0), axis=2, keepdims=True), packed.shape
        )
        for q in range(7)
    ]
    norm0 = jnp.sum(left2 + guess * (2.0 * cross + guess * square), axis=0)
    energy0 = jnp.sum(cross + guess * square, axis=0)
    alpha0 = norm0 / energy0
    off = guess - alpha0[None]
    norm1 = jnp.sum(left2 + off * (2.0 * cross + off * square), axis=0)
    energy1 = jnp.sum(energy + off * (mixed + off * second), axis=0)
    beta = norm1 / norm0
    alpha1 = norm1 / (energy1 - beta * norm1 / alpha0)
    scales[0] = alpha0 + alpha1 * (1.0 + beta)
    scales[1] = -alpha1 * alpha0
    for kl in range(16):
        one = scales[0, kl : kl + 1, :]
        two = scales[1, kl : kl + 1, :]
        out_ref[:, kl] = one * field_ref[:, kl] + two * shared_ref[:, kl]


def final(field, shared, sums):
    return pl.pallas_call(
        final_kernel,
        out_shape=jax.ShapeDtypeStruct(FIELD, F32),
        scratch_shapes=[pltpu.VMEM((2, 16, 128), F32)],
        compiler_params=pltpu.CompilerParams(vmem_limit_bytes=NARROW),
        cost_estimate=SMALL,
        name="pressure",
    )(field, shared, sums)


def swap_edges(edges):
    count = lax.axis_size("elem")
    far = [pair for i in range(1, count - 1, 2) for pair in ((i, i + 1), (i + 1, i))]
    far = lax.ppermute(edges, "elem", far)
    near = lax.ppermute(edges, "elem", [(i, i ^ 1) for i in range(count)])
    return near, far


def gather_sums(sums):
    count = lax.axis_size("elem")
    for step in (1, 2, 4):
        other = lax.ppermute(sums, "elem", [(i, i ^ step) for i in range(count)])
        sums = jnp.concatenate([sums, other], axis=0)
    return sums


def over(array, axis):
    return lax.all_to_all(array, axis, split_axis=0, concat_axis=0, tiled=True)


def per_device(velocity, metric, mass, sponge_rate, sponge_mask, neighbours):
    left = [jnp.asarray(t) for t in left_tables()]

    blocks = over(to_blocks(velocity), "mode")
    blocks, raw = in_planes(blocks, metric, sponge_rate, sponge_mask.reshape(1, 128), mass)
    raw = over(raw, "mode")
    blocks, raw = lax.optimization_barrier((blocks, raw))
    blocks = over(blocks, "mode")
    raw, edges = right_side(raw)
    near, far = swap_edges(edges)
    field, image, edges = image_of(raw, near, far, neighbours, metric, mass, left)
    near, far = swap_edges(edges)
    shared, sums = moments_of(image, near, far, field, neighbours, metric, mass, left)
    return from_blocks(blocks), final(field, shared, gather_sums(sums))


def solution(mesh):
    return jax.shard_map(
        per_device,
        mesh=mesh,
        in_specs=(
            P(None, None, "mode", None, "elem"),
            P(None, None, "elem"),
            P(None, "elem"),
            P(None, "elem"),
            P("elem"),
            P(None, "elem"),
        ),
        out_specs=(P(None, None, "mode", None, "elem"), P(None, "mode", None, "elem")),
        check_vma=False,
    )
```

```python
import jax
import jax.numpy as jnp
import ml_dtypes
import numpy as np
from jax import lax
from jax.experimental import pallas as pl
from jax.experimental.pallas import tpu as pltpu
from jax.sharding import PartitionSpec as P

F32 = jnp.float32
BF16 = jnp.bfloat16
MIB = 1024 * 1024
WIDE = 48 * MIB
BLOCKS = (16, 3, 128, 128)
NARROW = 16 * MIB
SMALL = pl.CostEstimate(flops=1000, bytes_accessed=1000, transcendentals=0)


def cheb_matrix():
    count = 8
    places = np.arange(count)
    points = np.cos(np.pi * places / (count - 1))
    weights = np.where((places == 0) | (places == count - 1), 2.0, 1.0)
    signs = weights * (-1.0) ** places
    differ = points[:, None] - points[None, :] + np.eye(count)
    table = np.outer(signs, 1.0 / signs) / differ
    table = table - np.eye(count) * np.sum(table, axis=1)[:, None]
    return table.astype(np.float32).astype(np.float64)


def two_parts(table):
    high = table.astype(np.float32).astype(ml_dtypes.bfloat16)
    low = (table - high.astype(np.float64)).astype(np.float32).astype(ml_dtypes.bfloat16)
    return high, low


def mode_order(modes):
    row = np.arange(modes)
    return 16 * ((row % (modes // 2)) // 8) + 2 * (row % 8) + row // (modes // 2)


def tables(modes):
    planes = 2 * modes
    half = modes // 2
    order = mode_order(modes)
    even, odd = order[:half], order[half:]
    spots = np.arange(half)

    def angles(places, ks):
        return ((places[:, None] * ks[None, :]) % planes) * (2.0 * np.pi / planes)

    quarter = np.array([half])
    weight_even = np.where(even == 0, 1.0, 2.0)
    extra = np.zeros((16, half))
    extra[:1] = weight_even * np.cos(angles(quarter, even))
    cos_even = np.concatenate([weight_even * np.cos(angles(spots, even)), extra], axis=0)
    cos_odd = 2.0 * np.cos(angles(spots, odd))
    sin_even = weight_even * np.sin(angles(spots, even))
    sin_odd = 2.0 * np.sin(angles(spots, odd))
    sin_odd[:1] = 2.0 * np.sin(angles(quarter, odd))
    back_cos_even = np.cos(angles(spots, even)).T / planes
    back_cos_odd = np.cos(angles(spots, odd)).T / planes
    back_sin_even = -np.sin(angles(spots, even)).T / planes
    back_sin_odd = -np.sin(angles(spots, odd)).T / planes
    back_sin_odd[:, :1] = -np.sin(angles(quarter, odd)).T / planes
    wave = np.broadcast_to((order * np.pi / modes)[:, None], (modes, 128)).astype(np.float32)
    sign = np.round(np.cos(angles(quarter, even)).T) / planes
    sign = np.broadcast_to(sign, (half, 128)).astype(np.float32)
    there = [cos_even, cos_odd, sin_even, sin_odd]
    back = [back_cos_even, back_cos_odd, back_sin_even, back_sin_odd]
    return there, back, wave, sign


def right_tables():
    table = cheb_matrix()
    two = np.eye(2)
    eight = np.eye(8)
    along_r = np.kron(two, np.kron(eight, table.T))
    along_s = np.kron(two, np.kron(table.T, eight))
    high, low = two_parts(np.concatenate([along_r, along_s], axis=1))
    return np.concatenate([high, high, low], axis=0)


def left_tables():
    table = cheb_matrix()
    eight = np.eye(8)
    along_r = np.kron(eight, table)
    along_s = np.kron(table, eight)
    high, low = two_parts(np.concatenate([along_r, along_s], axis=0))
    forward = np.concatenate([high, high, low], axis=1)
    high, low = two_parts(np.concatenate([along_r.T, along_s.T], axis=1))
    return forward, np.concatenate([high, high], axis=1), low


def split(value):
    high = value.astype(BF16)
    low = (value - high.astype(F32)).astype(BF16)
    return high, low


def dot(first, second):
    return jnp.dot(first, second, preferred_element_type=F32)


def low_half(shape):
    return lax.broadcasted_iota(jnp.int32, shape, len(shape) - 1) < 64


def swap(value):
    return pltpu.roll(value, 64, 1)


def spot(kl):
    return 8 * (kl % 2) + kl // 2


def pre_kernel(v_all, y_ref, v_ref, sems):
    def fetch(c, h):
        part = pl.ds(8 * h, 8)
        return pltpu.make_async_copy(v_all.at[c, :, part], v_ref.at[c, :, part], sems.at[c, h])

    pieces = [(c, h) for c in range(3) for h in range(2)]
    for piece in pieces:
        fetch(*piece).start()
    for c, h in pieces:
        fetch(c, h).wait()
        for kl in range(8 * h, 8 * h + 8):
            turned = v_ref[c, :, kl].reshape(128, 128).T
            for g in range(16):
                y_ref[g, c, pl.ds(spot(kl), 8, stride=16), :] = turned[8 * g : 8 * g + 8, :]


def to_blocks(velocity):
    return pl.pallas_call(
        pre_kernel,
        in_specs=[pl.BlockSpec(memory_space=pl.ANY)],
        out_specs=pl.BlockSpec(memory_space=pltpu.VMEM),
        out_shape=jax.ShapeDtypeStruct(BLOCKS, F32),
        scratch_shapes=[pltpu.VMEM((3, 2, 16, 64, 128), F32), pltpu.SemaphoreType.DMA((3, 2))],
        compiler_params=pltpu.CompilerParams(vmem_limit_bytes=48 * MIB),
        name="to_blocks",
    )(velocity)


ROWS = 32
LAG = 26


def node_rows(rows, tmp, metric_ref, rate_ref, mask_ref, mass_ref):
    place = pl.multiple_of(lax.axis_index("mode") * 8, 8)
    damping = mask_ref[...].astype(F32) * rate_ref[...]
    blank = jnp.zeros((64, 128), F32)
    values = [metric_ref[0], metric_ref[1], metric_ref[2], metric_ref[3], damping, mass_ref[...]]
    for q, value in enumerate(values):
        tmp[q] = jnp.concatenate([value, blank], axis=0).T
    for q in range(6):
        mine = tmp[q, pl.ds(place, 8), :]
        other = swap(mine)
        for i in range(4):
            row = mine[2 * i : 2 * i + 1, :] + other[2 * i + 1 : 2 * i + 2, :]
            rows[i // 2, q : q + 1, 128 * (i % 2) : 128 * (i % 2) + 128] = row


def stacked(high, low):
    return jnp.concatenate([high, low, high], axis=0)


def plane_kernel(
    z_all, metric_ref, rate_ref, mask_ref, mass_ref, wave_ref, sign_ref, slope_ref, ce_ref, co_ref,
    se_ref, so_ref, bce_ref, bco_ref, bse_ref, bso_ref, out_all, raw_ref, z_ref, out_ref, high, low, planes, eh, el,
    tail, grads, flat, rows_all, turned, z_sem,
    out_sem,
):
    def fetch(i, c):
        part = pl.ds(64 * i, 64)
        return pltpu.make_async_copy(z_all.at[:, c, part, :], z_ref.at[:, c, part, :], z_sem.at[i, c])

    def store(i):
        part = pl.ds(64 * i, 64)
        return pltpu.make_async_copy(out_ref.at[i], out_all.at[:, :, part, :], out_sem.at[i])

    for i in range(2):
        for c in range(3):
            fetch(i, c).start()
    node_rows(rows_all, turned, metric_ref, rate_ref, mask_ref, mass_ref)

    def one_half(i):
        return half_kernel(
            i, fetch, store, z_ref, wave_ref, sign_ref, slope_ref, ce_ref, co_ref, se_ref, so_ref, bce_ref, bco_ref,
            bse_ref, bso_ref, out_ref.at[i], raw_ref, high.at[i], low.at[i], planes.at[i], eh.at[i], el.at[i], tail.at[i],
            grads.at[i], flat.at[i], rows_all,
        )

    ahead, behind = one_half(0), one_half(1)
    for _ in range(LAG):
        next(ahead, None)
    running = [ahead, behind]
    while running:
        running = [half for half in running if next(half, "end") != "end"]
    for i in range(2):
        store(i).wait()


def half_kernel(
    i, fetch, store, z_ref, wave_ref, sign_ref, slope_ref, ce_ref, co_ref, se_ref, so_ref, bce_ref, bco_ref,
    bse_ref, bso_ref, out_ref, raw_ref, high, low, planes, eh, el, tail, grads, flat, rows_all,
):
    base = 64 * i
    node = rows_all[i]
    rx = node[0:1, :]
    ry = node[1:2, :]
    sx = node[2:3, :]
    sy = node[3:4, :]
    damping = node[4:5, :]
    mass = node[5:6, :]
    half = low_half((256, 128))

    def trade(first, second):
        return jnp.where(half, first, swap(second)), jnp.where(half, swap(first), second)

    def cells(c, place):
        return jnp.concatenate(
            [z_ref[:, c, pl.ds(base + place + 8 * p, 8), :].reshape(128, 128) for p in range(2)], axis=0
        )

    def slopes(c, part, q, up, down):
        cols = slice(128 * q, 128 * q + 128)
        both = dot(jnp.concatenate([up, down, up], axis=1), slope_ref[...])
        grads[c, part, 0, :, cols] = both[:, :128]
        grads[c, part, 1, :, cols] = both[:, 128:]

    for c in range(3):
        fetch(i, c).wait()
        for q in range(2):
            cols = slice(128 * q, 128 * q + 128)
            for part, value in enumerate(trade(cells(c, 32 * q), cells(c, 32 * q + 16))):
                if c < 2:
                    flat[c, part, :, cols] = value
                up, down = split(value)
                high[c, part, :, cols] = up
                low[c, part, :, cols] = down
            yield
    for c in range(3):
        for part in range(2):
            for q in range(2):
                cols = slice(128 * q, 128 * q + 128)
                slopes(c, part, q, high[c, part, :, cols], low[c, part, :, cols])
                yield

    for step in range(256 // ROWS):
        rows = slice(step * ROWS, step * ROWS + ROWS)
        wave = twice(wave_ref[rows, :])
        for part in range(2):
            u_r, u_s = grads[0, part, 0, rows, :], grads[0, part, 1, rows, :]
            v_r, v_s = grads[1, part, 0, rows, :], grads[1, part, 1, rows, :]
            w_r, w_s = grads[2, part, 0, rows, :], grads[2, part, 1, rows, :]
            u_t = flat[0, 1 - part, rows, :]
            v_t = flat[1, 1 - part, rows, :]
            turn = -wave if part == 0 else wave
            swirl = (
                ry * w_r + sy * w_s - turn * v_t,
                turn * u_t - (rx * w_r + sx * w_s),
                rx * v_r + sx * v_s - (ry * u_r + sy * u_s),
            )
            for c in range(3):
                up, down = split(swirl[c])
                high[3 + c, part, rows, :] = up
                low[3 + c, part, rows, :] = down
        yield

    for c in range(6):
        ce = dot(ce_ref[...], stacked(high[c, 0, :128], low[c, 0, :128]))
        co = dot(co_ref[...], stacked(high[c, 0, 128:], low[c, 0, 128:]))
        se = dot(se_ref[...], stacked(high[c, 1, :128], low[c, 1, :128]))
        so = dot(so_ref[...], stacked(high[c, 1, 128:], low[c, 1, 128:]))
        top, bottom = ce[:128] + co, ce[:128] - co
        add, sub = se + so, se - so
        planes[c, 0] = top - add
        planes[c, 1] = top + add
        planes[c, 2] = bottom + sub
        planes[c, 3] = bottom - sub
        planes[c, 0, 0:1, :] = ce[0:1] + co[0:1]
        planes[c, 1, 0:1, :] = ce[128:129] - so[0:1]
        planes[c, 2, 0:1, :] = ce[0:1] - co[0:1]
        planes[c, 3, 0:1, :] = ce[128:129] + so[0:1]
        yield

    def force(u, w):
        return (
            u[1] * w[2] - u[2] * w[1] - damping * (u[0] - 1.0),
            u[2] * w[0] - u[0] * w[2] - damping * u[1],
            u[0] * w[1] - u[1] * w[0] - damping * u[2],
        )

    first_row = lax.broadcasted_iota(jnp.int32, (ROWS, 256), 0) == 0
    for step in range(128 // ROWS):
        rows = slice(step * ROWS, step * ROWS + ROWS)
        quads = []
        for quad in range(4):
            here = [planes[c, quad, rows, :] for c in range(6)]
            quads.append(force(here[:3], here[3:]))
        for c in range(3):
            one, two, three, four = [quad[c] for quad in quads]
            plus, minus = one + two, one - two
            more, less = three + four, three - four
            sums = [plus + more, plus - more, minus - less, minus + less]
            if step == 0:
                sums[0] = jnp.where(first_row, one + three, sums[0])
                sums[1] = jnp.where(first_row, one - three, sums[1])
                sums[3] = jnp.where(first_row, two - four, sums[3])
                tail[c, 0:8, :] = (two + four)[0:8, :]
            for quad in range(4):
                up, down = split(sums[quad])
                eh[c, quad, rows, :] = up
                el[c, quad, rows, :] = down
        yield

    backs = (bce_ref, bco_ref, bse_ref, bso_ref)
    for c in range(3):
        for quad in range(4):
            value = dot(backs[quad][...], stacked(eh[c, quad], el[c, quad]))
            if quad == 0:
                value = value + twice(sign_ref[...]) * tail[c, 0:1, :]
            flat[c, quad // 2, 128 * (quad % 2) : 128 * (quad % 2) + 128, :] = value
            yield
    def put(ref, place, value):
        for p in range(2):
            ref[:, pl.ds(place + 8 * p, 8), :] = value[128 * p : 128 * p + 128].reshape(16, 8, 128)

    for c in range(3):
        for q in range(2):
            cols = slice(128 * q, 128 * q + 128)
            first, second = trade(flat[c, 0, :, cols], flat[c, 1, :, cols])
            put(out_ref.at[:, c], 32 * q, first)
            put(out_ref.at[:, c], 32 * q + 16, second)
            yield
    store(i).start()
    for c in range(2):
        for part in range(2):
            for q in range(2):
                slopes(c, part, q, *split(flat[c, part, :, 128 * q : 128 * q + 128]))
                yield

    x_r, x_s, y_r, y_s = -mass * rx, -mass * sx, -mass * ry, -mass * sy
    for q in range(2):
        cols = slice(128 * q, 128 * q + 128)
        values = []
        for part in range(2):
            turn = wave_ref[...] if part == 0 else -wave_ref[...]
            values.append(
                x_r[:, cols] * grads[0, part, 0, :, cols]
                + x_s[:, cols] * grads[0, part, 1, :, cols]
                + y_r[:, cols] * grads[1, part, 0, :, cols]
                + y_s[:, cols] * grads[1, part, 1, :, cols]
                + mass[:, cols] * (turn * flat[2, 1 - part, :, cols])
            )
        first, second = trade(*values)
        put(raw_ref, base + 32 * q, first)
        put(raw_ref, base + 32 * q + 16, second)
        yield


def in_planes(blocks, metric, rate, mask, mass):
    there, back, wave, sign = tables(256)
    consts = [wave, sign, right_tables()]
    for table in there + back:
        high, low = two_parts(table)
        consts.append(np.concatenate([high, high, low], axis=1))
    consts = [jnp.asarray(c) for c in consts]

    in_vmem = pl.BlockSpec(memory_space=pltpu.VMEM)
    return pl.pallas_call(
        plane_kernel,
        in_specs=[pl.BlockSpec(memory_space=pl.ANY)] + [in_vmem] * (4 + len(consts)),
        out_specs=[pl.BlockSpec(memory_space=pl.ANY), in_vmem],
        out_shape=[
            jax.ShapeDtypeStruct(BLOCKS, F32),
            jax.ShapeDtypeStruct((16, 128, 128), F32),
        ],
        scratch_shapes=[
            pltpu.VMEM(BLOCKS, F32),
            pltpu.VMEM((2, 16, 3, 64, 128), F32),
            pltpu.VMEM((2, 6, 2, 256, 256), BF16),
            pltpu.VMEM((2, 6, 2, 256, 256), BF16),
            pltpu.VMEM((2, 6, 4, 128, 256), F32),
            pltpu.VMEM((2, 3, 4, 128, 256), BF16),
            pltpu.VMEM((2, 3, 4, 128, 256), BF16),
            pltpu.VMEM((2, 3, 8, 256), F32),
            pltpu.VMEM((2, 3, 2, 2, 256, 256), F32),
            pltpu.VMEM((2, 3, 2, 256, 256), F32),
            pltpu.VMEM((2, 8, 256), F32),
            pltpu.VMEM((6, 128, 128), F32),
            pltpu.SemaphoreType.DMA((2, 3)),
            pltpu.SemaphoreType.DMA((2,)),
        ],
        compiler_params=pltpu.CompilerParams(vmem_limit_bytes=50 * MIB),
        name="in_planes",
    )(blocks, metric, rate, mask, mass, *consts)


def slopes_of(pair, forward):
    up, down = split(pair)
    both = dot(forward, jnp.concatenate([up, down, up], axis=0))
    return both[:64], both[64:]


def twice(value):
    return jnp.concatenate([value, value], axis=1)


FIELD = (2, 16, 64, 128)
EDGE = (2, 2, 16, 8, 128)


def whole_spec(shape):
    return pl.BlockSpec(shape, lambda i: (0,) * len(shape))


def wave_of(kl):
    return (lax.axis_index("mode") * 16 + kl).astype(F32) * (np.pi / 256)


def right_kernel(r_ref, raw_ref, edge_ref):
    for kl in range(16):
        block = jnp.concatenate([r_ref[g, pl.ds(spot(kl), 8, stride=16), :] for g in range(16)], axis=0)
        raw_ref[:, kl] = block.T.reshape(2, 64, 128)
        for part in range(2):
            edge_ref[0, part, kl] = raw_ref[part, kl, pl.ds(0, 8, stride=8), :]
            edge_ref[1, part, kl] = raw_ref[part, kl, pl.ds(7, 8, stride=8), :]


def right_side(blocks):
    return pl.pallas_call(
        right_kernel,
        out_shape=[jax.ShapeDtypeStruct(FIELD, F32), jax.ShapeDtypeStruct(EDGE, F32)],
        compiler_params=pltpu.CompilerParams(vmem_limit_bytes=NARROW),
        cost_estimate=SMALL,
        name="right_side",
    )(blocks)


def post_kernel(r_ref, non_all, non_ref, sems):
    def store(c, h):
        part = pl.ds(8 * h, 8)
        return pltpu.make_async_copy(non_ref.at[c, :, part], non_all.at[c, :, part], sems.at[c, h])

    pieces = [(c, h) for c in range(3) for h in range(2)]
    for c, h in pieces:
        for kl in range(8 * h, 8 * h + 8):
            block = jnp.concatenate([r_ref[g, c, pl.ds(spot(kl), 8, stride=16), :] for g in range(16)], axis=0)
            non_ref[c, :, kl] = block.T.reshape(2, 64, 128)
        store(c, h).start()
    for piece in pieces:
        store(*piece).wait()


def from_blocks(blocks):
    return pl.pallas_call(
        post_kernel,
        in_specs=[pl.BlockSpec(memory_space=pltpu.VMEM)],
        out_specs=pl.BlockSpec(memory_space=pl.ANY),
        out_shape=jax.ShapeDtypeStruct((3, 2, 16, 64, 128), F32),
        scratch_shapes=[pltpu.VMEM((3, 2, 16, 64, 128), F32), pltpu.SemaphoreType.DMA((3, 2))],
        compiler_params=pltpu.CompilerParams(vmem_limit_bytes=NARROW),
        name="from_blocks",
    )(blocks)


def lanes(value, index):
    return jnp.take_along_axis(value, index, axis=1, mode="promise_in_bounds")


def links_of(link_ref):
    device = lax.axis_index("elem")
    links = []
    for side in range(4):
        ident = jnp.broadcast_to(link_ref[side : side + 1, :], (8, 128))
        here = ident >= 0
        if side < 2:
            place = ident - (device - 1) * 128
            origin = place >> 7
            origin = jnp.where((device & 1) == 1, origin, 2 - origin)
            links.append((jnp.where(here, place & 127, 0), jnp.where(here, origin, 3)))
        else:
            links.append((jnp.where(here, ident - device * 128, 0), here))
    return links


def share(out_ref, field_ref, near_edge, far_edge, links, part, kl):
    (west_lane, west_from), (east_lane, east_from), (south_lane, south_here), (north_lane, north_here) = links
    first = field_ref[part, kl, pl.ds(0, 8, stride=8), :]
    last = field_ref[part, kl, pl.ds(7, 8, stride=8), :]

    def pick(side, own, lane, origin):
        value = jnp.where(origin == 1, lanes(own, lane), 0.0)
        value = jnp.where(origin == 0, lanes(near_edge[side, part, kl], lane), value)
        return jnp.where(origin == 2, lanes(far_edge[side, part, kl], lane), value)

    out_ref[part, kl] = field_ref[part, kl]
    out_ref[part, kl, pl.ds(0, 8, stride=8), :] = first + pick(1, last, west_lane, west_from)
    out_ref[part, kl, pl.ds(7, 8, stride=8), :] = last + pick(0, first, east_lane, east_from)
    bottom = out_ref[part, kl, 0:8, :]
    top = out_ref[part, kl, 56:64, :]
    out_ref[part, kl, 0:8, :] = bottom + jnp.where(south_here, lanes(top, south_lane), 0.0)
    out_ref[part, kl, 56:64, :] = top + jnp.where(north_here, lanes(bottom, north_lane), 0.0)


def set_stiff(stiff, metric_ref, mass_ref):
    mass = mass_ref[...]
    rx, ry, sx, sy = metric_ref[0], metric_ref[1], metric_ref[2], metric_ref[3]
    stiff[0] = mass * (rx * rx + ry * ry)
    stiff[1] = mass * (rx * sx + ry * sy)
    stiff[2] = mass * (sx * sx + sy * sy)


def set_inverse(inverse, link_ref):
    node = lax.broadcasted_iota(jnp.int32, (64, 128), 0)
    here = [link_ref[side : side + 1, :] >= 0 for side in range(4)]
    places = [(node & 7) == 0, (node & 7) == 7, node < 8, node >= 56]
    value = jnp.ones((64, 128), F32)
    for place, there in zip(places, here):
        value = jnp.where(place & there, 0.5 * value, value)
    inverse[...] = value


def stiffness(pair, shift, stiff, mass_ref, fwd_ref, adj_ref, adl_ref):
    along_r, along_s = slopes_of(pair, fwd_ref[...])
    cross = twice(stiff[1])
    back = jnp.concatenate(
        [
            twice(stiff[0]) * along_r + cross * along_s,
            cross * along_r + twice(stiff[2]) * along_s,
        ],
        axis=0,
    )
    up, down = split(back)
    folded = dot(adj_ref[...], jnp.concatenate([up, down], axis=0)) + dot(adl_ref[...], up)
    return folded + shift * twice(mass_ref[...]) * pair


def image_kernel(
    raw_ref, near_edge, far_edge, link_ref, metric_ref, mass_ref, fwd_ref, adj_ref, adl_ref,
    field_ref, image_ref, edge_ref, stiff,
):
    links = links_of(link_ref)
    set_stiff(stiff, metric_ref, mass_ref)
    for kl in range(16):
        for part in range(2):
            share(field_ref, raw_ref, near_edge, far_edge, links, part, kl)
    for kl in range(16):
        pair = jnp.concatenate([field_ref[0, kl], field_ref[1, kl]], axis=1)
        wave = wave_of(kl)
        image = stiffness(pair, wave * wave + 1.0, stiff, mass_ref, fwd_ref, adj_ref, adl_ref)
        for part in range(2):
            image_ref[part, kl] = image[:, 128 * part : 128 * part + 128]
            edge_ref[0, part, kl] = image_ref[part, kl, pl.ds(0, 8, stride=8), :]
            edge_ref[1, part, kl] = image_ref[part, kl, pl.ds(7, 8, stride=8), :]


def image_of(raw, near, far, links, metric, mass, left):
    return pl.pallas_call(
        image_kernel,
        in_specs=[pl.BlockSpec(memory_space=pltpu.VMEM)] * 9,
        out_shape=[
            jax.ShapeDtypeStruct(FIELD, F32),
            jax.ShapeDtypeStruct(FIELD, F32),
            jax.ShapeDtypeStruct(EDGE, F32),
        ],
        scratch_shapes=[pltpu.VMEM((3, 64, 128), F32)],
        compiler_params=pltpu.CompilerParams(vmem_limit_bytes=NARROW),
        cost_estimate=SMALL,
        name="image",
    )(raw, near, far, links, metric, mass, *left)


def folded_rows(value):
    return jnp.sum(value[0] + value[1], axis=0, keepdims=True)


def moments_kernel(
    image_ref, near_edge, far_edge, field_ref, link_ref, metric_ref, mass_ref, fwd_ref, adj_ref,
    adl_ref, shared_ref, sum_ref, stiff, inverse, second, rows, local,
):
    links = links_of(link_ref)
    set_stiff(stiff, metric_ref, mass_ref)
    set_inverse(inverse, link_ref)
    for kl in range(16):
        for part in range(2):
            share(shared_ref, image_ref, near_edge, far_edge, links, part, kl)
    for kl in range(16):
        pair = jnp.concatenate([shared_ref[0, kl], shared_ref[1, kl]], axis=1)
        wave = wave_of(kl)
        image = stiffness(pair, wave * wave + 1.0, stiff, mass_ref, fwd_ref, adj_ref, adl_ref)
        for part in range(2):
            second[part, kl] = image[:, 128 * part : 128 * part + 128]
        weighed = shared_ref[:, kl] * inverse[...]
        rows[0, kl : kl + 1, :] = folded_rows(weighed * field_ref[:, kl])
        rows[1, kl : kl + 1, :] = folded_rows(weighed * shared_ref[:, kl])
    cross = jnp.sum(rows[0], axis=1, keepdims=True)
    square = jnp.sum(rows[1], axis=1, keepdims=True)
    guess = jnp.where(square > 0.0, cross / jnp.where(square > 0.0, square, 1.0), 0.0)
    local[...] = jnp.broadcast_to(guess, (16, 128))
    for kl in range(16):
        step = local[kl : kl + 1, :]
        one = shared_ref[:, kl]
        two = second[:, kl]
        left = field_ref[:, kl] - step * one
        image = image_ref[:, kl] - step * two
        weighed = left * inverse[...]
        rows[0, kl : kl + 1, :] = folded_rows(left * weighed)
        rows[2, kl : kl + 1, :] = folded_rows(one * weighed)
        rows[3, kl : kl + 1, :] = folded_rows(left * image)
        rows[4, kl : kl + 1, :] = folded_rows(left * two + one * image)
        rows[5, kl : kl + 1, :] = folded_rows(one * two)
    place = lax.broadcasted_iota(jnp.int32, (16, 128), 1)
    packed = local[...]
    for q, row in enumerate((0, 2, 1, 3, 4, 5)):
        packed = jnp.where(place == q + 1, jnp.sum(rows[row], axis=1, keepdims=True), packed)
    sum_ref[0] = packed


def moments_of(image, near, far, field, links, metric, mass, left):
    return pl.pallas_call(
        moments_kernel,
        in_specs=[pl.BlockSpec(memory_space=pltpu.VMEM)] * 10,
        out_shape=[jax.ShapeDtypeStruct(FIELD, F32), jax.ShapeDtypeStruct((1, 16, 128), F32)],
        scratch_shapes=[
            pltpu.VMEM((3, 64, 128), F32),
            pltpu.VMEM((64, 128), F32),
            pltpu.VMEM(FIELD, F32),
            pltpu.VMEM((6, 16, 128), F32),
            pltpu.VMEM((16, 128), F32),
        ],
        compiler_params=pltpu.CompilerParams(vmem_limit_bytes=NARROW),
        cost_estimate=SMALL,
        name="moments",
    )(image, near, far, field, links, metric, mass, *left)


def final_kernel(field_ref, shared_ref, sum_ref, out_ref, scales):
    packed = sum_ref[...]
    place = lax.broadcasted_iota(jnp.int32, packed.shape, 2)
    guess, left2, cross, square, energy, mixed, second = [
        jnp.broadcast_to(
            jnp.sum(jnp.where(place == q, packed, 0.0), axis=2, keepdims=True), packed.shape
        )
        for q in range(7)
    ]
    norm0 = jnp.sum(left2 + guess * (2.0 * cross + guess * square), axis=0)
    energy0 = jnp.sum(cross + guess * square, axis=0)
    alpha0 = norm0 / energy0
    off = guess - alpha0[None]
    norm1 = jnp.sum(left2 + off * (2.0 * cross + off * square), axis=0)
    energy1 = jnp.sum(energy + off * (mixed + off * second), axis=0)
    beta = norm1 / norm0
    alpha1 = norm1 / (energy1 - beta * norm1 / alpha0)
    scales[0] = alpha0 + alpha1 * (1.0 + beta)
    scales[1] = -alpha1 * alpha0
    for kl in range(16):
        one = scales[0, kl : kl + 1, :]
        two = scales[1, kl : kl + 1, :]
        out_ref[:, kl] = one * field_ref[:, kl] + two * shared_ref[:, kl]


def final(field, shared, sums):
    return pl.pallas_call(
        final_kernel,
        out_shape=jax.ShapeDtypeStruct(FIELD, F32),
        scratch_shapes=[pltpu.VMEM((2, 16, 128), F32)],
        compiler_params=pltpu.CompilerParams(vmem_limit_bytes=NARROW),
        cost_estimate=SMALL,
        name="pressure",
    )(field, shared, sums)


def swap_edges(edges):
    count = lax.axis_size("elem")
    far = [pair for i in range(1, count - 1, 2) for pair in ((i, i + 1), (i + 1, i))]
    far = lax.ppermute(edges, "elem", far)
    near = lax.ppermute(edges, "elem", [(i, i ^ 1) for i in range(count)])
    return near, far


def gather_sums(sums):
    count = lax.axis_size("elem")
    for step in (1, 2, 4):
        other = lax.ppermute(sums, "elem", [(i, i ^ step) for i in range(count)])
        sums = jnp.concatenate([sums, other], axis=0)
    return sums


def over(array, axis):
    return lax.all_to_all(array, axis, split_axis=0, concat_axis=0, tiled=True)


def per_device(velocity, metric, mass, sponge_rate, sponge_mask, neighbours):
    left = [jnp.asarray(t) for t in left_tables()]

    blocks = over(to_blocks(velocity), "mode")
    blocks, raw = in_planes(blocks, metric, sponge_rate, sponge_mask.reshape(1, 128), mass)
    raw = over(raw, "mode")
    blocks, raw = lax.optimization_barrier((blocks, raw))
    blocks = over(blocks, "mode")
    raw, edges = right_side(raw)
    near, far = swap_edges(edges)
    field, image, edges = image_of(raw, near, far, neighbours, metric, mass, left)
    near, far = swap_edges(edges)
    shared, sums = moments_of(image, near, far, field, neighbours, metric, mass, left)
    return from_blocks(blocks), final(field, shared, gather_sums(sums))


def solution(mesh):
    return jax.shard_map(
        per_device,
        mesh=mesh,
        in_specs=(
            P(None, None, "mode", None, "elem"),
            P(None, None, "elem"),
            P(None, "elem"),
            P(None, "elem"),
            P("elem"),
            P(None, "elem"),
        ),
        out_specs=(P(None, None, "mode", None, "elem"), P(None, "mode", None, "elem")),
        check_vma=False,
    )
```
